32 devices in a mesh: section: 4 (over z), dp: 8 (over y, x, core).
Axes of the slice: x: 2, y: 2, z: 4, core: 2. Of those that a mesh axis runs over, the one named last changes fastest.
Arguments:
- output_gradient: bfloat16 [4, 1024, 2048], P('section', 'dp'), may hold values from -6 to 6
- saved_input: bfloat16 [4, 1024, 8192], P('section', 'dp'), may hold values from -6 to 6
- frozen_matrix: bfloat16 [4, 8192, 2048], P('section', 'dp'), may hold values from -0.0625 to 0.0625
- adapter_down_maps: bfloat16 [4, 8192, 512], P('section', None, 'dp'), may hold values from -0.0625 to 0.0625
- adapter_up_maps: bfloat16 [4, 2048, 512], P('section', None, 'dp'), may hold values from -0.125 to 0.125
- token_tenants: int32 [4, 1024], P('section'), may hold values from 0 to 7, never falling along the last dimension, each value on 1 to 256 neighbouring positions
- tenant_slot_lookup: int32 [4, 8], P('section'), may hold values from 0 to 7, each once within a row
Outputs:
- passed_grad: bfloat16 [4, 1024, 8192], P('section', 'dp')
- down_gradient: bfloat16 [4, 8192, 512], P('section', None, 'dp')
- up_gradient: bfloat16 [4, 2048, 512], P('section', None, 'dp')
The draws below stay inside these ranges and needn't reach their ends.
Inputs may be any that keep to these rules, and one draw needn't show every extreme that they name: `token_tenants`: within a section the ids never fall; each of the 8 tenants has 1 to 256 tokens, one exactly 256. `tenant_slot_lookup`: each section's row is a permutation.
All inputs are finite; a program needn't handle non-finite values.
Results may differ from the reference program's by a relative error of at most 0.005.
Values may be sent and summed in bfloat16 or wider, within the bound.
No kernel may reach another device: no remote copies, remote signals or barrier semaphores. Data moves between devices by JAX's collectives and lax.ppermute only.
A program may use at most 128 MiB of HBM per device.

```python
import math
import jax
import jax.numpy as jnp
import numpy as np

MODEL_WIDTH = 8192
KEY_VALUE_WIDTH = 2048
ADAPTER_RANK = 64
RELAY_SECTIONS = 4
TOKENS = 1024
TENANT_COUNT = 8
MOST = 256


def block_levels(stream_key, extent, pieces, low, largest):
    factor_of, own = 1.0, jax.random.fold_in(stream_key, 6)
    for position, blocks in pieces:
        draws = jnp.exp(jax.random.uniform(jax.random.fold_in(own, position), (blocks,), jnp.float32, low / len(pieces), largest / len(pieces)))
        factor_of = factor_of * jnp.repeat(draws, extent[position] // blocks).reshape([-1 if axis == position else 1 for axis in range(len(extent))])
    return factor_of


def profile(number_of, total, reach, slope):
    loads = [(1 << 20) // math.isqrt(grade ** slope) + 1 for grade in range(2, number_of + 1)]
    rest, holding = total - reach - (number_of - 1), [1] * (number_of - 1)
    while rest > 0:
        free = [i for i in range(number_of - 1) if holding[i] < reach]
        mass, left = sum([loads[i] for i in free]), rest
        for i in free:
            addition = min(reach - holding[i], max(1, left * loads[i] // mass), rest)
            holding[i] = holding[i] + addition
            rest = rest - addition
    return np.array([reach] + holding)


def uneven(stream_key, number_of, total, limit, skew):
    if number_of == 2:
        one = jax.random.randint(stream_key, (), max(1, total - limit), min(limit, total - 1) + 1)
        return jnp.stack([one, total - one])
    sizes = jnp.asarray(profile(number_of, total, limit, skew), jnp.int32)
    couples = (number_of - 1) // 2
    giver, taker = sizes[1:1 + 2 * couples:2], sizes[2:2 + 2 * couples:2]
    slack = jnp.minimum(giver - 1, limit - taker)
    shifted = jax.random.randint(jax.random.fold_in(stream_key, 1), (couples,), 0, 1 << 20) % (slack + 1)
    sizes = sizes.at[1:1 + 2 * couples:2].set(giver - shifted).at[2:2 + 2 * couples:2].set(taker + shifted)
    return sizes[jax.random.permutation(jax.random.fold_in(stream_key, 2), number_of)]


def noise(own_key, shape, deviation, bound, pieces=(), held_as=jnp.bfloat16):
    gain = block_levels(own_key, shape, pieces, -0.22, 0.18) if pieces else 1.0
    array = jax.random.normal(own_key, shape, jnp.float32) * deviation * gain
    return jnp.minimum(jnp.maximum(array, -bound), bound).astype(held_as)


def setup_inputs(seed: int = 0) -> dict:
    splits = jax.random.split(jax.random.key(seed), 8)
    return {
        "output_gradient": noise(splits[0], (RELAY_SECTIONS, TOKENS, KEY_VALUE_WIDTH), 1.0, 6.0, ((0, 4), (1, 8))),
        "saved_input": noise(splits[1], (RELAY_SECTIONS, TOKENS, MODEL_WIDTH), 1.0, 6.0, ((0, 4), (1, 8))),
        "frozen_matrix": noise(splits[2], (RELAY_SECTIONS, MODEL_WIDTH, KEY_VALUE_WIDTH), MODEL_WIDTH ** -0.5, 0.0625, ((0, 4), (1, 8))),
        "adapter_down_maps": noise(splits[3], (RELAY_SECTIONS, MODEL_WIDTH, TENANT_COUNT * ADAPTER_RANK), MODEL_WIDTH ** -0.5, 0.0625, ((0, 4), (2, 8))),
        "adapter_up_maps": noise(splits[4], (RELAY_SECTIONS, KEY_VALUE_WIDTH, TENANT_COUNT * ADAPTER_RANK), KEY_VALUE_WIDTH ** -0.5, 0.125, ((0, 4), (2, 8))),
        "token_tenants": jax.vmap(lambda own: jnp.searchsorted(jnp.cumsum(uneven(own, TENANT_COUNT, TOKENS, MOST, 2)), jnp.arange(TOKENS), side="right"))(jax.random.split(splits[5], RELAY_SECTIONS)).reshape((RELAY_SECTIONS, TOKENS)).astype(jnp.int32),
        "tenant_slot_lookup": jax.vmap(lambda own: jax.random.permutation(own, TENANT_COUNT))(jax.random.split(splits[6], RELAY_SECTIONS)).reshape((RELAY_SECTIONS, TENANT_COUNT)).astype(jnp.int32),
    }


adapter_scale = 2.0


def block_layout(tenant_row, slot_table, tenants, most):
    tokens = tenant_row.shape[0]
    tenant_range = jnp.arange(tenants, dtype=jnp.int32)
    member = (tenant_range[:, None] == tenant_row[None, :]).astype(jnp.int32)
    counts = jnp.sum(member, axis=1).astype(jnp.int32)
    starts = (jnp.cumsum(counts).astype(jnp.int32) - counts).astype(jnp.int32)
    owner_match = (slot_table[None, :] == tenant_range[:, None]).astype(jnp.int32)
    slot_start = jnp.sum(owner_match * starts[None, :], axis=1).astype(jnp.int32)
    slot_count = jnp.sum(owner_match * counts[None, :], axis=1).astype(jnp.int32)
    place = jnp.arange(most, dtype=jnp.int32)
    live_slot = place[None, :] < slot_count[:, None]
    row_index = jnp.minimum(slot_start[:, None] + place[None, :], tokens - 1).astype(jnp.int32)
    token_slot = jnp.sum(member * slot_table[:, None], axis=0).astype(jnp.int32)
    token_start = jnp.sum(member * starts[:, None], axis=0).astype(jnp.int32)
    token_place = (token_slot * most + jnp.arange(tokens, dtype=jnp.int32) - token_start).astype(jnp.int32)
    return row_index, live_slot, token_place


def masked_rows(rows, row_index, live_slot):
    picked = rows[row_index]
    return jnp.where(live_slot[:, :, None], picked, jnp.zeros((), picked.dtype))


def section_gradients(grad_rows, saved_rows, weight, down_maps, up_maps, tenant_row, slot_table):
    row_index, live_slot, token_place = block_layout(tenant_row, slot_table, TENANT_COUNT, MOST)
    gradient_blocks = masked_rows(grad_rows, row_index, live_slot).astype(jnp.float32)
    saved_input_blocks = masked_rows(saved_rows, row_index, live_slot).astype(jnp.float32)
    down_three = down_maps.reshape(MODEL_WIDTH, TENANT_COUNT, ADAPTER_RANK).astype(jnp.float32)
    up_three = up_maps.reshape(KEY_VALUE_WIDTH, TENANT_COUNT, ADAPTER_RANK).astype(jnp.float32)
    rank_up_values = jnp.einsum("kpe,ekr->kpr", gradient_blocks, up_three).astype(jnp.bfloat16)
    rank_down_values = jnp.einsum("kpd,dkr->kpr", saved_input_blocks, down_three).astype(jnp.bfloat16)
    adapter_blocks = jnp.einsum("kpr,dkr->kpd", rank_up_values.astype(jnp.float32), down_three)
    adapter_slot = adapter_blocks.reshape(TENANT_COUNT * MOST, MODEL_WIDTH)[token_place]
    frozen_product = jnp.dot(grad_rows, weight.T, preferred_element_type=jnp.float32)
    input_gradient = (frozen_product + adapter_scale * adapter_slot).astype(jnp.bfloat16)
    down_gradient = (adapter_scale * jnp.einsum("tfv,tfy->vty", saved_input_blocks, rank_up_values.astype(jnp.float32))).reshape(MODEL_WIDTH, TENANT_COUNT * ADAPTER_RANK).astype(jnp.bfloat16)
    up_gradient = (adapter_scale * jnp.einsum("ohz,ohq->zoq", gradient_blocks, rank_down_values.astype(jnp.float32))).reshape(KEY_VALUE_WIDTH, TENANT_COUNT * ADAPTER_RANK).astype(jnp.bfloat16)
    return input_gradient, down_gradient, up_gradient


def reference(output_gradient, saved_input, frozen_matrix, adapter_down_maps, adapter_up_maps, token_tenants, tenant_slot_lookup):
    inputs_all = []
    downs_all = []
    ups_all = []
    for section_index in range(RELAY_SECTIONS):
        input_gradient, down_gradient, up_gradient = section_gradients(output_gradient[section_index], saved_input[section_index], frozen_matrix[section_index], adapter_down_maps[section_index], adapter_up_maps[section_index], token_tenants[section_index], tenant_slot_lookup[section_index])
        inputs_all.append(input_gradient)
        downs_all.append(down_gradient)
        ups_all.append(up_gradient)
    stacked = jnp.stack(inputs_all)
    passed_grad = jnp.concatenate([stacked[1:], jnp.zeros_like(stacked[:1])], axis=0)
    return passed_grad, jnp.stack(downs_all), jnp.stack(ups_all)
```

```python
import functools

import jax
import jax.numpy as jnp
from jax import lax
from jax.experimental import pallas as pl
from jax.experimental.pallas import tpu as pltpu
from jax.sharding import PartitionSpec as P

ADAPTER_RANK = 64
MOST = 256
VMEM_BYTES = 56 * 1024 * 1024

adapter_scale = 2.0

NT = (((1,), (1,)), ((), ()))
TN = (((0,), (0,)), ((), ()))
NN = (((1,), (0,)), ((), ()))

ANY = pl.BlockSpec(memory_space=pl.ANY)
SMEM = pl.BlockSpec(memory_space=pltpu.SMEM)
VMEM = pl.BlockSpec(memory_space=pltpu.VMEM)


def partner(value, distance):
    count = lax.axis_size("dp")
    return lax.ppermute(value, "dp", [(i, i ^ distance) for i in range(count)])


def to_previous(value, distance):
    sections, count = lax.axis_size("section"), lax.axis_size("dp")
    pairs = [
        (s * count + i, (s - 1) * count + (i ^ distance))
        for s in range(1, sections)
        for i in range(count)
    ]
    return lax.ppermute(value, ("section", "dp"), pairs)


def slot_ranges(tenant_row, slot_table):
    tenants = slot_table.shape[0]
    ids = jnp.arange(tenants, dtype=jnp.int32)
    counts = jnp.sum((tenant_row[None, :] == ids[:, None]).astype(jnp.int32), axis=1)
    starts = jnp.sum((tenant_row[None, :] < ids[:, None]).astype(jnp.int32), axis=1)
    owner = slot_table[None, :] == ids[:, None]
    slot_start = jnp.sum(jnp.where(owner, starts[None, :], 0), axis=1)
    slot_count = jnp.sum(jnp.where(owner, counts[None, :], 0), axis=1)
    return slot_start, slot_count


def copy_window(me, first, same_ref, other_ref, window_ref, sem, wide):
    block = same_ref.shape[1]
    for i in range(wide):
        relative = jnp.bitwise_xor(me, first + i)
        chip, core = lax.shift_right_logical(relative, 1), jnp.bitwise_and(relative, 1)
        target = window_ref.at[pl.ds(i * block, block)]

        @pl.when(core == 0)
        def _():
            pltpu.make_async_copy(same_ref.at[chip], target, sem.at[i]).start()

        @pl.when(core == 1)
        def _():
            pltpu.make_async_copy(other_ref.at[chip], target, sem.at[i]).start()

    for i in range(wide):
        target = window_ref.at[pl.ds(i * block, block)]
        pltpu.make_async_copy(same_ref.at[0], target, sem.at[i]).wait()


def owned(meta_ref, slots, block, width):
    me = meta_ref[3 * slots]
    start, count, first = meta_ref[me], meta_ref[slots + me], meta_ref[2 * slots + me]
    token = first * block + lax.broadcasted_iota(jnp.int32, (1, width), 1)
    return (token >= start) & (token < start + count)


def rank_up_kernel(slots, wide, meta_ref, up_ref, same_ref, other_ref, out_ref, window_ref, sem):
    block = same_ref.shape[1]
    me = meta_ref[3 * slots]
    copy_window(me, meta_ref[2 * slots + me], same_ref, other_ref, window_ref, sem, wide)
    product = lax.dot_general(
        up_ref[...], window_ref[...], NT, preferred_element_type=jnp.float32
    )
    product = jnp.where(owned(meta_ref, slots, block, wide * block), product, 0.0)
    product = product.astype(out_ref.dtype)
    for i in range(wide):
        out_ref[i] = product[:, i * block : (i + 1) * block]


def spread(meta_ref, slots, first_slot, count, token_block, wins_ref, out_ref, column):
    rank, block = wins_ref.shape[3], wins_ref.shape[4]
    wide = wins_ref.shape[2]
    me = meta_ref[3 * slots]
    for row in range(count):
        slot = first_slot + row
        relative = jnp.bitwise_xor(me, slot)
        place = token_block - meta_ref[2 * slots + slot]
        inside = (place >= 0) & (place < wide)
        value = wins_ref[
            jnp.bitwise_and(relative, 1),
            lax.shift_right_logical(relative, 1),
            jnp.clip(place, 0, wide - 1),
        ]
        out_ref[pl.ds(row * rank, rank), pl.ds(column, block)] = jnp.where(
            inside, value, jnp.zeros_like(value)
        )


def input_kernel(slots, chip, meta_ref, same_ref, other_ref, wins_ref, down_ref, out_ref, rows_ref):
    block = out_ref.shape[1]
    me = meta_ref[3 * slots]
    for core in range(2):
        token_block = jnp.bitwise_xor(me, 2 * chip + core)
        spread(meta_ref, slots, 0, slots, token_block, wins_ref, rows_ref, core * block)
    term = lax.dot_general(rows_ref[...], down_ref[...], TN, preferred_element_type=jnp.float32)
    out_ref[0] = (same_ref[0] + adapter_scale * term[:block]).astype(out_ref.dtype)
    out_ref[1] = (other_ref[0] + adapter_scale * term[block:]).astype(out_ref.dtype)


def feature_kernel(slots, group, meta_ref, saved_ref, down_ref, wins_ref, v_ref, grad_ref, rows_ref, part_ref):
    wide, rank, block = v_ref.shape[1], v_ref.shape[2], v_ref.shape[3]
    first_slot = pl.program_id(0) * group
    blocks = saved_ref.shape[0] // block
    for token_block in range(blocks):
        spread(
            meta_ref, slots, first_slot, group, token_block, wins_ref, rows_ref, token_block * block
        )
    part = lax.dot_general(
        down_ref[...], saved_ref[...], NT, preferred_element_type=jnp.float32
    ).astype(v_ref.dtype)
    for token_block in range(blocks):
        part_ref[token_block] = part[:, token_block * block : (token_block + 1) * block]
    for row in range(group):
        first = meta_ref[2 * slots + first_slot + row]
        for i in range(wide):
            v_ref[row, i] = part_ref[first + i, pl.ds(row * rank, rank), :]
    grad = lax.dot_general(rows_ref[...], saved_ref[...], NN, preferred_element_type=jnp.float32)
    grad = (adapter_scale * grad).astype(grad_ref.dtype)
    for row in range(group):
        grad_ref[row] = grad[row * rank : (row + 1) * rank]


def up_kernel(slots, wide, meta_ref, v_ref, same_ref, other_ref, out_ref, window_ref, sem):
    block = same_ref.shape[1]
    me = meta_ref[3 * slots]
    copy_window(me, meta_ref[2 * slots + me], same_ref, other_ref, window_ref, sem, wide)
    total = jnp.sum(v_ref[...].astype(jnp.float32), axis=0)
    values = jnp.concatenate([total[i] for i in range(wide)], axis=1)
    values = jnp.where(owned(meta_ref, slots, block, wide * block), values, 0.0)
    product = lax.dot_general(
        values.astype(jnp.bfloat16), window_ref[...], NN, preferred_element_type=jnp.float32
    )
    out_ref[...] = (adapter_scale * product).astype(out_ref.dtype)


def assemble_kernel(pieces, me_ref, *refs):
    piece_refs, out_ref, sem = refs[:pieces], refs[pieces], refs[pieces + 1]
    width = piece_refs[0].shape[1]
    copies = []
    for k in range(pieces):
        column = pl.multiple_of(jnp.bitwise_xor(me_ref[0], k) * width, width)
        copies.append(
            pltpu.make_async_copy(piece_refs[k], out_ref.at[:, pl.ds(column, width)], sem.at[k])
        )
    for copy in copies:
        copy.start()
    for copy in copies:
        copy.wait()


def params(**more):
    return pltpu.CompilerParams(vmem_limit_bytes=VMEM_BYTES, **more)


def local(
    output_gradient,
    saved_input,
    frozen_matrix,
    adapter_down_maps,
    adapter_up_maps,
    token_tenants,
    tenant_slot_lookup,
):
    grad_rows = output_gradient[0]
    saved_rows = saved_input[0]
    weight = frozen_matrix[0]
    down_local = adapter_down_maps[0].T
    up_local = adapter_up_maps[0].T
    slots = tenant_slot_lookup.shape[1]
    block, out_width = grad_rows.shape
    local_width = weight.shape[0]
    count = lax.axis_size("dp")
    chips = count // 2
    wide = -(-MOST // block) + 1
    me = lax.axis_index("dp").astype(jnp.int32)
    bf16, f32 = jnp.bfloat16, jnp.float32

    slot_start, slot_count = slot_ranges(token_tenants[0], tenant_slot_lookup[0])
    first = jnp.minimum(slot_start // block, count - wide)
    meta = jnp.concatenate([slot_start, slot_count, first, me[None]]).astype(jnp.int32)

    same = jnp.stack([grad_rows] + [partner(grad_rows, 2 * c) for c in range(1, chips)])
    other = partner(same, 1)
    down_cols = lax.all_to_all(down_local, "dp", split_axis=1, concat_axis=0, tiled=True)

    window = pltpu.VMEM((wide * block, out_width), bf16)
    window_sem = pltpu.SemaphoreType.DMA((wide,))
    u_window = pl.pallas_call(
        functools.partial(rank_up_kernel, slots, wide),
        out_shape=jax.ShapeDtypeStruct((wide, ADAPTER_RANK, block), bf16),
        in_specs=[SMEM, VMEM, ANY, ANY],
        out_specs=VMEM,
        scratch_shapes=[window, window_sem],
        compiler_params=params(),
        name="rank_up",
    )(meta, up_local, same, other)
    u_same = jnp.stack([u_window] + [partner(u_window, 2 * c) for c in range(1, chips)])
    wins = jnp.stack([u_same, partner(u_same, 1)])

    def frozen(rows):
        flat = rows.reshape(chips * block, out_width)
        product = lax.dot_general(flat, weight, NT, preferred_element_type=f32)
        return product.reshape(chips, block, local_width)

    frozen_same, frozen_other = frozen(same), frozen(other)
    pieces = [None] * count
    for c in range(chips):
        chip_rows = pl.BlockSpec((1, block, local_width), lambda i, c=c: (c, 0, 0))
        whole = lambda shape: pl.BlockSpec(shape, lambda i: (0,) * len(shape))
        grads = pl.pallas_call(
            functools.partial(input_kernel, slots, c),
            grid=(1,),
            out_shape=jax.ShapeDtypeStruct((2, block, local_width), bf16),
            in_specs=[SMEM, chip_rows, chip_rows, whole(wins.shape), whole(down_cols.shape)],
            out_specs=whole((2, block, local_width)),
            scratch_shapes=[pltpu.VMEM((slots * ADAPTER_RANK, 2 * block), bf16)],
            compiler_params=params(),
            name="input_grad",
        )(meta, frozen_same, frozen_other, wins, down_cols)
        if c:
            grads = partner(grads, 2 * c)
        for core in range(2):
            pieces[2 * c + core] = to_previous(grads[core], core)
    passed = pl.pallas_call(
        functools.partial(assemble_kernel, count),
        out_shape=jax.ShapeDtypeStruct((block, count * local_width), bf16),
        in_specs=[SMEM] + [ANY] * count,
        out_specs=ANY,
        scratch_shapes=[pltpu.SemaphoreType.DMA((count,))],
        compiler_params=params(),
        name="assemble",
    )(me[None], *pieces)

    saved_cols = lax.all_to_all(saved_rows, "dp", split_axis=1, concat_axis=0, tiled=True)
    group = min(slots, 8)
    tokens = count * block
    v_windows, down_grads = pl.pallas_call(
        functools.partial(feature_kernel, slots, group),
        grid=(slots // group,),
        out_shape=[
            jax.ShapeDtypeStruct((slots, wide, ADAPTER_RANK, block), bf16),
            jax.ShapeDtypeStruct((slots, ADAPTER_RANK, local_width), bf16),
        ],
        in_specs=[
            SMEM,
            pl.BlockSpec((tokens, local_width), lambda i: (0, 0)),
            pl.BlockSpec((group * ADAPTER_RANK, local_width), lambda i: (i, 0)),
            pl.BlockSpec(wins.shape, lambda i: (0,) * 5),
        ],
        out_specs=[
            pl.BlockSpec((group, wide, ADAPTER_RANK, block), lambda i: (i, 0, 0, 0)),
            pl.BlockSpec((group, ADAPTER_RANK, local_width), lambda i: (i, 0, 0)),
        ],
        scratch_shapes=[
            pltpu.VMEM((group * ADAPTER_RANK, tokens), bf16),
            pltpu.VMEM((count, group * ADAPTER_RANK, block), bf16),
        ],
        compiler_params=params(),
        name="feature",
    )(meta, saved_cols, down_cols, wins)
    down_gradient = lax.all_to_all(down_grads, "dp", split_axis=0, concat_axis=2, tiled=True)[0]
    v_all = lax.all_to_all(v_windows, "dp", split_axis=0, concat_axis=0, tiled=True)
    up_gradient = pl.pallas_call(
        functools.partial(up_kernel, slots, wide),
        out_shape=jax.ShapeDtypeStruct((ADAPTER_RANK, out_width), bf16),
        in_specs=[SMEM, VMEM, ANY, ANY],
        out_specs=VMEM,
        scratch_shapes=[window, window_sem],
        compiler_params=params(),
        name="up_grad",
    )(meta, v_all, same, other)
    return (passed[None], down_gradient.T[None], up_gradient.T[None])


def solution(mesh):
    return jax.shard_map(
        local,
        mesh=mesh,
        in_specs=(
            P("section", "dp", None),
            P("section", "dp", None),
            P("section", "dp", None),
            P("section", None, "dp"),
            P("section", None, "dp"),
            P("section", None),
            P("section", None),
        ),
        out_specs=(P("section", "dp", None), P("section", None, "dp"), P("section", None, "dp")),
        check_vma=False,
    )
```

```python
import functools
import math

import jax
import jax.numpy as jnp
from jax import lax
from jax.experimental import pallas as pl
from jax.experimental.pallas import tpu as pltpu
from jax.sharding import PartitionSpec as P

ADAPTER_RANK = 64
MOST = 256
MIB = 1024 * 1024

adapter_scale = 2.0

NT = (((1,), (1,)), ((), ()))
TN = (((0,), (0,)), ((), ()))
NN = (((1,), (0,)), ((), ()))

ANY = pl.BlockSpec(memory_space=pl.ANY)
SMEM = pl.BlockSpec(memory_space=pltpu.SMEM)
VMEM = pl.BlockSpec(memory_space=pltpu.VMEM)


def partner(value, distance):
    count = lax.axis_size("dp")
    return lax.ppermute(value, "dp", [(i, i ^ distance) for i in range(count)])


def chip_partner(value, order):
    count = lax.axis_size("dp")
    if count == 8 and order in (1, 2):
        pairs = [(i, i ^ (2 if (i + order) % 2 else 4)) for i in range(count)]
        return lax.ppermute(value, "dp", pairs)
    return partner(value, 2 * order) if order else value


def swapped(order, count):
    return 3 - order if count == 8 and order in (1, 2) else order


def devices_in_order(me, count):
    out = []
    for order in range(count // 2):
        distance = jnp.int32(2 * order)
        if count == 8 and order in (1, 2):
            distance = jnp.where((me + order) % 2 == 1, 2, 4)
        out += [me ^ distance, me ^ distance ^ 1]
    return jnp.stack(out).astype(jnp.int32)


def after(value, *others):
    return lax.optimization_barrier((value, *others))[0]


def to_previous(value, distance):
    sections, count = lax.axis_size("section"), lax.axis_size("dp")
    pairs = [
        (s * count + i, (s - 1) * count + (i ^ distance))
        for s in range(1, sections)
        for i in range(count)
    ]
    return lax.ppermute(value, ("section", "dp"), pairs)


def slot_ranges(tenant_row, slot_table):
    tenants = slot_table.shape[0]
    ids = jnp.arange(tenants, dtype=jnp.int32)
    counts = jnp.sum((tenant_row[None, :] == ids[:, None]).astype(jnp.int32), axis=1)
    starts = jnp.sum((tenant_row[None, :] < ids[:, None]).astype(jnp.int32), axis=1)
    owner = slot_table[None, :] == ids[:, None]
    slot_start = jnp.sum(jnp.where(owner, starts[None, :], 0), axis=1)
    slot_count = jnp.sum(jnp.where(owner, counts[None, :], 0), axis=1)
    return slot_start, slot_count


def pick(index, refs, act):
    for k, ref in enumerate(refs):

        @pl.when(index == k)
        def _():
            act(ref)


def device_at(meta_ref, slots, place):
    return meta_ref[3 * slots + 1 + place]


def place_of(meta_ref, slots, device):
    return meta_ref[4 * slots + 1 + device]


def owned(meta_ref, slots, first_token, width):
    me = meta_ref[3 * slots]
    start, count = meta_ref[me], meta_ref[slots + me]
    token = first_token + lax.broadcasted_iota(jnp.int32, (1, width), 1)
    return (token >= start) & (token < start + count)


def split_kernel(slots, meta_ref, in_ref, own_ref, across_ref):
    chips, _, width = own_ref.shape
    for order in range(chips):
        to_own = meta_ref[2 * order]
        to_other = meta_ref[2 * swapped(order, slots) + 1]
        for device, out_ref in ((to_own, own_ref), (to_other, across_ref)):
            out_ref[order] = in_ref[:, pl.ds(pl.multiple_of(device * width, width), width)]


def frozen_kernel(same_ref, other_ref, weight_ref, out_ref):
    rows = jnp.concatenate([same_ref[...], other_ref[...]], axis=0)
    out_ref[...] = lax.dot_general(rows, weight_ref[...], NT, preferred_element_type=jnp.float32)


def rank_rows(slots, chip, meta_ref, up_ref, same_ref, other_ref):
    block = same_ref.shape[0]
    values = []
    for core, ref in enumerate((same_ref, other_ref)):
        first_token = device_at(meta_ref, slots, 2 * chip + core) * block
        product = lax.dot_general(up_ref[...], ref[...], NT, preferred_element_type=jnp.float32)
        product = jnp.where(owned(meta_ref, slots, first_token, block), product, 0.0)
        values.append(product.astype(jnp.bfloat16))
    return values


def rank_kernel(slots, chip, meta_ref, up_ref, same_ref, other_ref, out_ref):
    for core, value in enumerate(rank_rows(slots, chip, meta_ref, up_ref, same_ref, other_ref)):
        out_ref[core] = value


def last_rank_kernel(slots, chips, meta_ref, up_ref, same_ref, other_ref, *refs):
    before_refs, (out_ref, all_ref) = refs[: chips - 1], refs[chips - 1 :]
    for c, ref in enumerate(before_refs):
        all_ref[pl.ds(2 * c, 2)] = ref[...]
    last = rank_rows(slots, chips - 1, meta_ref, up_ref, same_ref, other_ref)
    for core, value in enumerate(last):
        all_ref[2 * (chips - 1) + core] = value
    me = meta_ref[3 * slots]
    for i in range(out_ref.shape[0]):
        out_ref[i] = all_ref[place_of(meta_ref, slots, meta_ref[2 * slots + me] + i)]


def spread(meta_ref, slots, rows, token_block, wins_refs, out_ref, column):
    _, wide, rank, block = wins_refs[0].shape
    for row, k in enumerate(rows):
        place = token_block - meta_ref[2 * slots + device_at(meta_ref, slots, k)]
        inside = (place >= 0) & (place < wide)
        order = swapped(k // 2, slots) if k % 2 else k // 2
        value = wins_refs[k % 2][order, jnp.clip(place, 0, wide - 1)]
        out_ref[pl.ds(row * rank, rank), pl.ds(column, block)] = jnp.where(
            inside, value, jnp.zeros_like(value)
        )


def input_kernel(slots, orders, meta_ref, same_ref, other_ref, down_ref, *refs):
    frozen_refs, (out_ref, rows_ref) = refs[: len(orders)], refs[len(orders) :]
    block = frozen_refs[0].shape[0] // 2
    for i, order in enumerate(orders):
        for core in range(2):
            token_block = device_at(meta_ref, slots, 2 * order + core)
            column = (2 * i + core) * block
            spread(
                meta_ref, slots, range(slots), token_block, (same_ref, other_ref), rows_ref, column
            )
    term = lax.dot_general(rows_ref[...], down_ref[...], TN, preferred_element_type=jnp.float32)
    for i, frozen_ref in enumerate(frozen_refs):
        part = term[2 * i * block : 2 * (i + 1) * block]
        total = (frozen_ref[...] + adapter_scale * part).astype(out_ref.dtype)
        out_ref[i, 0], out_ref[i, 1] = total[:block], total[block:]


def feature_kernel(
    slots, rows, meta_ref, saved_ref, down_ref, same_ref, other_ref, out_ref, rows_ref, v_ref
):
    rank, block = v_ref.shape[1:]
    width = saved_ref.shape[1]
    blocks = v_ref.shape[0]

    def spread_block(token_block, carry):
        column = token_block * block
        if not isinstance(column, int):
            column = pl.multiple_of(column, block)
        spread(meta_ref, slots, rows, token_block, (same_ref, other_ref), rows_ref, column)
        return carry

    lax.fori_loop(0, blocks, spread_block, 0, unroll=blocks <= 8)
    down = down_ref[pl.ds(rows[0] * rank, len(rows) * rank), :]
    part = lax.dot_general(down, saved_ref[...], NT, preferred_element_type=jnp.float32)
    ranges = []
    for k in rows:
        slot = device_at(meta_ref, slots, k)
        ranges.append((meta_ref[slot], meta_ref[slot] + meta_ref[slots + slot]))
    for token_block in range(blocks):
        lane = slice(token_block * block, (token_block + 1) * block)
        token = token_block * block + lax.broadcasted_iota(jnp.int32, (1, block), 1)
        value = jnp.zeros((rank, block), jnp.float32) if rows[0] == 0 else v_ref[token_block]
        for row, (start, stop) in enumerate(ranges):
            inside = (token >= start) & (token < stop)
            value = jnp.where(inside, part[row * rank : (row + 1) * rank, lane], value)
        v_ref[token_block] = value
    grad = lax.dot_general(rows_ref[...], saved_ref[...], NN, preferred_element_type=jnp.float32)
    grad = (adapter_scale * grad).astype(out_ref.dtype)
    for row, k in enumerate(rows):
        slot = device_at(meta_ref, slots, k)
        out_ref[slot, :, pl.ds(0, width)] = grad[row * rank : (row + 1) * rank]


def all_features_kernel(slots, group, *refs):
    for start in range(0, slots, group):
        feature_kernel(slots, range(start, min(start + group, slots)), *refs)
    saved_ref, out_ref, v_ref = refs[1], refs[5], refs[7]
    width, block = saved_ref.shape[1], v_ref.shape[2]
    value = v_ref[...]
    near = value.astype(out_ref.dtype)
    out_ref[:, :, pl.ds(width, block)] = near
    rest = value - near.astype(jnp.float32)
    out_ref[:, :, pl.ds(width + block, block)] = rest.astype(out_ref.dtype)


def merge_kernel(mixed_ref, down_ref, v_ref):
    count = mixed_ref.shape[0]
    block = v_ref.shape[1]
    width = mixed_ref.shape[2] - 2 * block
    total = jnp.zeros(v_ref.shape, jnp.float32)
    for source in range(count):
        down_ref[:, source * width : (source + 1) * width] = mixed_ref[source, :, pl.ds(0, width)]
        for part in range(2):
            value = mixed_ref[source, :, pl.ds(width + part * block, block)]
            total = total + value.astype(jnp.float32)
    v_ref[...] = total.astype(v_ref.dtype)


def window_kernel(slots, count, meta_ref, *refs):
    row_refs, (out_ref, sem) = refs[:count], refs[count:]
    block = row_refs[0].shape[0]
    wide = out_ref.shape[0] // block
    first = meta_ref[2 * slots + meta_ref[3 * slots]]
    for i in range(wide):
        target = out_ref.at[pl.ds(i * block, block)]
        pick(
            place_of(meta_ref, slots, first + i),
            row_refs,
            lambda ref: pltpu.make_async_copy(ref, target, sem.at[i]).start(),
        )
    for i in range(wide):
        target = out_ref.at[pl.ds(i * block, block)]
        pltpu.make_async_copy(row_refs[0], target, sem.at[i]).wait()


def up_kernel(slots, meta_ref, same_ref, other_ref, window_ref, out_ref):
    block = same_ref.shape[2]
    span = window_ref.shape[0]
    me = meta_ref[3 * slots]
    first = meta_ref[2 * slots + me]
    values = []
    for i in range(span // block):
        place = place_of(meta_ref, slots, first + i)
        order = lax.shift_right_logical(place, 1)
        mirror = order
        if slots == 8:
            mirror = jnp.where((order == 1) | (order == 2), 3 - order, order)
        value = jnp.where(jnp.bitwise_and(place, 1) == 0, same_ref[order], other_ref[mirror])
        values.append(value)
    values = jnp.concatenate(values, axis=1)
    values = jnp.where(owned(meta_ref, slots, first * block, span), values, jnp.zeros_like(values))
    product = lax.dot_general(values, window_ref[...], NN, preferred_element_type=jnp.float32)
    out_ref[...] = (adapter_scale * product).astype(out_ref.dtype)


def regroup_kernel(in_ref, out_ref):
    width = out_ref.shape[2]
    for k in range(out_ref.shape[0]):
        out_ref[k] = in_ref[:, k * width : (k + 1) * width]


def assemble_kernel(slots, meta_ref, *refs):
    chips = slots // 2
    own_refs, other_refs, (out_ref, sem) = refs[:chips], refs[chips:slots], refs[slots:]
    width = own_refs[0].shape[-1]
    copies = []
    for order in range(chips):
        own_ref = own_refs[order].at[0]
        other_ref = other_refs[order] if order else other_refs[order].at[1]
        other = 2 * swapped(order, slots) + 1
        for source, ref in ((2 * order, own_ref), (other, other_ref)):
            column = pl.multiple_of(device_at(meta_ref, slots, source) * width, width)
            target = out_ref.at[:, pl.ds(column, width)]
            copies.append(pltpu.make_async_copy(ref, target, sem.at[len(copies)]))
    for copy in copies:
        copy.start()
    for copy in copies:
        copy.wait()


def local(
    output_gradient,
    saved_input,
    frozen_matrix,
    adapter_down_maps,
    adapter_up_maps,
    token_tenants,
    tenant_slot_lookup,
):
    grad_rows = output_gradient[0]
    saved_rows = saved_input[0]
    weight = frozen_matrix[0]
    down_local = adapter_down_maps[0].T
    up_local = adapter_up_maps[0].T
    slots = tenant_slot_lookup.shape[1]
    block, out_width = grad_rows.shape
    local_width = weight.shape[0]
    count = lax.axis_size("dp")
    chips = count // 2
    wide = -(-MOST // block) + 1
    me = lax.axis_index("dp").astype(jnp.int32)
    bf16, f32 = jnp.bfloat16, jnp.float32

    slot_start, slot_count = slot_ranges(token_tenants[0], tenant_slot_lookup[0])
    first = jnp.minimum(slot_start // block, count - wide)
    devices = devices_in_order(me, count)
    ids = jnp.arange(count, dtype=jnp.int32)
    places = jnp.sum(jnp.where(devices[None, :] == ids[:, None], ids[None, :], 0), axis=1)
    meta = [slot_start, slot_count, first, me[None], devices, places]
    meta = jnp.concatenate(meta).astype(jnp.int32)

    def call(kernel, name, out, operands, in_specs, out_specs, flops=0, scratch_shapes=()):
        arrays = list(operands) + (out if isinstance(out, list) else [out])
        held = sum(v.size * v.dtype.itemsize for v in arrays)
        held += sum(
            math.prod(v.shape) * jnp.dtype(v.dtype).itemsize
            for v in scratch_shapes
            if v.memory_space == pltpu.VMEM
        )
        return pl.pallas_call(
            kernel,
            out_shape=out,
            in_specs=in_specs,
            out_specs=out_specs,
            scratch_shapes=scratch_shapes,
            compiler_params=pltpu.CompilerParams(vmem_limit_bytes=min(60 * MIB, 2 * held + 4 * MIB)),
            name=name,
            cost_estimate=pl.CostEstimate(flops=0, bytes_accessed=0, transcendentals=0),
        )(*operands)

    def shape(*dims, dtype=bf16):
        return jax.ShapeDtypeStruct(dims, dtype)

    def rank_up(order, meta):
        return call(
            functools.partial(rank_kernel, slots, order),
            "rank_up",
            shape(2, ADAPTER_RANK, block),
            (meta, up_local, same[order], other[order]),
            [SMEM, VMEM, VMEM, VMEM],
            VMEM,
            flops=4 * block * out_width * ADAPTER_RANK,
        )

    def frozen_part(order, rows):
        return call(
            frozen_kernel,
            "frozen",
            shape(2 * block, local_width, dtype=f32),
            (rows, other[order], weight),
            [VMEM] * 3,
            VMEM,
            flops=4 * block * out_width * local_width,
        )

    def input_part(orders, meta):
        return call(
            functools.partial(input_kernel, slots, orders),
            "input_grad",
            shape(len(orders), 2, block, local_width),
            (meta, u_same, u_other, down_cols, *[frozen[order] for order in orders]),
            [SMEM] + [VMEM] * (3 + len(orders)),
            VMEM,
            flops=4 * len(orders) * block * slots * ADAPTER_RANK * local_width,
            scratch_shapes=[pltpu.VMEM((slots * ADAPTER_RANK, 2 * len(orders) * block), bf16)],
        )

    last = chips - 1
    same = [grad_rows, chip_partner(grad_rows, 1)]
    own_down, across_down = call(
        functools.partial(split_kernel, slots),
        "split_down",
        [shape(chips, ADAPTER_RANK, local_width)] * 2,
        (devices, down_local),
        [SMEM, VMEM],
        [VMEM, VMEM],
    )
    across_down = partner(across_down, 1)
    later_rows = after(grad_rows, own_down)
    same += [chip_partner(later_rows, order) for order in range(2, chips if chips != 4 else 3)]
    down_parts = [jnp.stack([own_down[order], across_down[order]]) for order in range(chips)]
    down_parts[1] = chip_partner(down_parts[1], 1)
    saved_pieces = call(
        regroup_kernel,
        "regroup_saved",
        shape(count, block, local_width),
        (after(saved_rows, across_down),),
        [VMEM],
        VMEM,
    )

    frozen = [None] * chips
    other = [partner(grad_rows, 1)]
    u_blocks = [rank_up(0, after(meta, across_down))]
    frozen[0] = frozen_part(0, after(same[0], u_blocks[0]))
    if chips == 4:
        same.append(chip_partner(after(same[1], across_down), 2))
    other += [partner(same[swapped(order, count)], 1) for order in range(1, last)]
    for order in range(2, chips):
        down_parts[order] = chip_partner(after(down_parts[order], same[1]), order)
    meta_now = after(meta, frozen[0], down_parts[1])
    for order in range(1, last):
        u_blocks.append(rank_up(order, meta_now))
        meta_now = after(meta, u_blocks[-1])
    frozen[1] = frozen_part(1, after(same[1], u_blocks[-1]))
    same[last] = after(same[last], frozen[1])
    other.append(partner(same[last], 1))
    u_window = call(
        functools.partial(last_rank_kernel, slots, chips),
        "rank_up_window",
        shape(wide, ADAPTER_RANK, block),
        (after(meta, down_parts[2]), up_local, same[-1], other[-1], *u_blocks),
        [SMEM] + [VMEM] * (2 + chips),
        VMEM,
        flops=4 * block * out_width * ADAPTER_RANK,
        scratch_shapes=[pltpu.VMEM((count, ADAPTER_RANK, block), bf16)],
    )
    u_parts = [chip_partner(u_window, order) for order in range(chips)]
    u_same = jnp.stack(u_parts)
    u_other = partner(u_same, 1)
    done = u_window
    for order in range(2, chips):
        frozen[order] = frozen_part(order, after(same[order], done))
        done = frozen[order]
    down_cols = jnp.stack(down_parts).reshape(slots * ADAPTER_RANK, local_width)

    saved_cols = lax.all_to_all(
        after(saved_pieces, done, *u_parts, down_cols), "dp", split_axis=0, concat_axis=0, tiled=True
    ).reshape(count * block, local_width)

    below = [None] * chips
    meta_now = meta
    for order in range(last, -1, -1):
        grads = input_part([order], meta_now)[0]
        meta_now = after(meta, grads)
        if order == 0:
            grads = jnp.stack([grads[0], partner(grads[1], 1)])
        below[order] = to_previous(grads, 0)

    group = min(slots, 8)
    tokens = count * block
    rows_in_order = [rows for pair in zip(same, other) for rows in pair]
    row_window = call(
        functools.partial(window_kernel, slots, count),
        "row_window",
        shape(wide * block, out_width),
        (meta_now, *rows_in_order),
        [SMEM] + [ANY] * count,
        ANY,
        scratch_shapes=[pltpu.SemaphoreType.DMA((wide,))],
    )
    mixed = call(
        functools.partial(all_features_kernel, slots, group),
        "feature",
        shape(slots, ADAPTER_RANK, local_width + 2 * block),
        (after(meta, row_window, below[last]), saved_cols, down_cols, u_same, u_other),
        [SMEM] + [VMEM] * 4,
        VMEM,
        flops=4 * tokens * slots * ADAPTER_RANK * local_width,
        scratch_shapes=[
            pltpu.VMEM((group * ADAPTER_RANK, tokens), bf16),
            pltpu.VMEM((count, ADAPTER_RANK, block), f32),
        ],
    )
    pieces = [[below[0], below[0]]]
    for order in range(1, chips):
        grads = chip_partner(below[order] if order == last else after(below[order], mixed), order)
        pieces.append([grads, partner(grads[1], 1)])
    passed = call(
        functools.partial(assemble_kernel, slots),
        "assemble",
        shape(block, count * local_width),
        (meta, *[own for own, _ in pieces], *[other for _, other in pieces]),
        [SMEM] + [VMEM] * count,
        ANY,
        scratch_shapes=[pltpu.SemaphoreType.DMA((count,))],
    )
    mixed = lax.all_to_all(mixed, "dp", split_axis=0, concat_axis=0, tiled=True)
    down_gradient, v_block = call(
        merge_kernel,
        "merge",
        [shape(ADAPTER_RANK, count * local_width), shape(ADAPTER_RANK, block)],
        (after(mixed, *[other for _, other in pieces[2:]]),),
        [VMEM],
        [VMEM, VMEM],
    )
    v_same = jnp.stack([chip_partner(v_block, order) for order in range(chips)])
    v_other = partner(v_same, 1)
    up_gradient = call(
        functools.partial(up_kernel, slots),
        "up_grad",
        shape(ADAPTER_RANK, out_width),
        (meta, v_same, v_other, row_window),
        [SMEM] + [VMEM] * 3,
        VMEM,
        flops=2 * wide * block * out_width * ADAPTER_RANK,
    )
    return (passed[None], down_gradient.T[None], up_gradient.T[None])


def solution(mesh):
    return jax.shard_map(
        local,
        mesh=mesh,
        in_specs=(
            P("section", "dp", None),
            P("section", "dp", None),
            P("section", "dp", None),
            P("section", None, "dp"),
            P("section", None, "dp"),
            P("section", None),
            P("section", None),
        ),
        out_specs=(P("section", "dp", None), P("section", None, "dp"), P("section", None, "dp")),
        check_vma=False,
    )
```

```python
import functools
import math

import jax
import jax.numpy as jnp
from jax import lax
from jax.experimental import pallas as pl
from jax.experimental.pallas import tpu as pltpu
from jax.sharding import PartitionSpec as P

ADAPTER_RANK = 64
MOST = 256
MIB = 1024 * 1024

adapter_scale = 2.0

NT = (((1,), (1,)), ((), ()))
TN = (((0,), (0,)), ((), ()))
NN = (((1,), (0,)), ((), ()))

ANY = pl.BlockSpec(memory_space=pl.ANY)
HBM = pl.BlockSpec(memory_space=pltpu.MemorySpace.HBM)
SMEM = pl.BlockSpec(memory_space=pltpu.SMEM)
VMEM = pl.BlockSpec(memory_space=pltpu.VMEM)


def partner(value, distance):
    count = lax.axis_size("dp")
    return lax.ppermute(value, "dp", [(i, i ^ distance) for i in range(count)])


def chip_partner(value, order):
    count = lax.axis_size("dp")
    if count == 8 and order in (1, 2):
        pairs = [(i, i ^ (2 if (i + order) % 2 else 4)) for i in range(count)]
        return lax.ppermute(value, "dp", pairs)
    return partner(value, 2 * order) if order else value


def swapped(order, count):
    return 3 - order if count == 8 and order in (1, 2) else order


def devices_in_order(me, count):
    out = []
    for order in range(count // 2):
        distance = jnp.int32(2 * order)
        if count == 8 and order in (1, 2):
            distance = jnp.where((me + order) % 2 == 1, 2, 4)
        out += [me ^ distance, me ^ distance ^ 1]
    return jnp.stack(out).astype(jnp.int32)


def corner(value):
    if value.size <= 1 << 17:
        return value
    rows = min(16, value.shape[-2])
    tile = value[(0,) * (value.ndim - 2)][:rows, :128] if value.ndim > 2 else value[:rows, :128]
    return tile


def in_place_kernel(*refs):
    pass


def after(value, *others):
    operands = [value, *map(corner, others)]
    return pl.pallas_call(
        in_place_kernel,
        out_shape=jax.ShapeDtypeStruct(value.shape, value.dtype),
        in_specs=[ANY] * len(operands),
        out_specs=ANY,
        input_output_aliases={0: 0},
        name="in_order",
    )(*operands)


def in_hbm(value):
    return pltpu.with_memory_space_constraint(value, pltpu.MemorySpace.HBM)


def to_previous(value, distance):
    sections, count = lax.axis_size("section"), lax.axis_size("dp")
    pairs = [
        (s * count + i, (s - 1) * count + (i ^ distance))
        for s in range(1, sections)
        for i in range(count)
    ]
    return lax.ppermute(value, ("section", "dp"), pairs)


def slot_ranges(tenant_row, slot_table):
    tenants = slot_table.shape[0]
    ids = jnp.arange(tenants, dtype=jnp.int32)
    counts = jnp.sum((tenant_row[None, :] == ids[:, None]).astype(jnp.int32), axis=1)
    starts = jnp.sum((tenant_row[None, :] < ids[:, None]).astype(jnp.int32), axis=1)
    owner = slot_table[None, :] == ids[:, None]
    slot_start = jnp.sum(jnp.where(owner, starts[None, :], 0), axis=1)
    slot_count = jnp.sum(jnp.where(owner, counts[None, :], 0), axis=1)
    return slot_start, slot_count


def pick(index, refs, act):
    for k, ref in enumerate(refs):

        @pl.when(index == k)
        def _():
            act(ref)


def device_at(meta_ref, slots, place):
    return meta_ref[3 * slots + 1 + place]


def place_of(meta_ref, slots, device):
    return meta_ref[4 * slots + 1 + device]


def owned(meta_ref, slots, first_token, width):
    me = meta_ref[3 * slots]
    start, count = meta_ref[me], meta_ref[slots + me]
    token = first_token + lax.broadcasted_iota(jnp.int32, (1, width), 1)
    return (token >= start) & (token < start + count)


def by_device(meta_ref, slots, device, same_ref, other_ref, *index):
    place = place_of(meta_ref, slots, device)
    order = lax.shift_right_logical(place, 1)
    mirror = order
    if slots == 8:
        mirror = jnp.where((order == 1) | (order == 2), 3 - order, order)
    own = jnp.bitwise_and(place, 1) == 0
    return jnp.where(own, same_ref[(order, *index)], other_ref[(mirror, *index)])


def gather_up_kernel(slots, meta_ref, *refs):
    row_refs, (out_ref, sem) = refs[:slots], refs[slots:]
    rank = out_ref.shape[0] // slots
    copies = []
    for k, ref in enumerate(row_refs):
        row = pl.multiple_of(device_at(meta_ref, slots, k) * rank, rank)
        source = ref.at[pl.ds(ref.shape[0] - rank, rank)]
        copies.append(pltpu.make_async_copy(source, out_ref.at[pl.ds(row, rank)], sem.at[k]))
    for copy in copies:
        copy.start()
    for copy in copies:
        copy.wait()


def input_kernel(slots, order, meta_ref, same_ref, other_ref, weight_ref, up_ref, down_ref, *refs):
    out_ref, all_u_ref, u_ref, sem = refs[-4:]
    block = out_ref.shape[1]
    rank = up_ref.shape[0] // slots
    rows = jnp.concatenate([same_ref[pl.ds(0, block)], other_ref[pl.ds(0, block)]], axis=0)
    u = lax.dot_general(rows, up_ref[...], NT, preferred_element_type=jnp.float32)
    lane = lax.broadcasted_iota(jnp.int32, (1, slots * rank), 1)
    start = jnp.zeros_like(lane)
    stop = jnp.zeros_like(lane)
    for slot in range(slots):
        first = meta_ref[slot]
        inside = lane >= slot * rank
        start = jnp.where(inside, first, start)
        stop = jnp.where(inside, first + meta_ref[slots + slot], stop)
    token = lax.broadcasted_iota(jnp.int32, (block, 1), 0)
    parts = []
    for core in range(2):
        here = token + device_at(meta_ref, slots, 2 * order + core) * block
        inside = (here >= start) & (here < stop)
        parts.append(jnp.where(inside, u[core * block : (core + 1) * block], 0.0).astype(u_ref.dtype))
        u_ref[core] = parts[core]
    copies = []
    for core in range(2):
        row = device_at(meta_ref, slots, 2 * order + core) * block
        target = all_u_ref.at[pl.ds(pl.multiple_of(row, block), block)]
        copies.append(pltpu.make_async_copy(u_ref.at[core], target, sem.at[core]))
        copies[core].start()
    total = lax.dot_general(rows, weight_ref[...], NT, preferred_element_type=jnp.float32)
    term = lax.dot_general(
        jnp.concatenate(parts, axis=0), down_ref[...], NN, preferred_element_type=jnp.float32
    )
    total = (total + adapter_scale * term).astype(out_ref.dtype)
    out_ref[0], out_ref[1] = total[:block], total[block:]
    for copy in copies:
        copy.wait()


def feature_kernel(slots, rows, meta_ref, saved_ref, down_ref, u_ref, out_ref, v_ref):
    rank, block = v_ref.shape[1:]
    width = saved_ref.shape[1]
    blocks = v_ref.shape[0]
    down = down_ref[pl.ds(rows[0] * rank, len(rows) * rank), :]
    part = lax.dot_general(down, saved_ref[...], NT, preferred_element_type=jnp.float32)
    ranges = []
    for slot in rows:
        ranges.append((meta_ref[slot], meta_ref[slot] + meta_ref[slots + slot]))
    for token_block in range(blocks):
        lane = slice(token_block * block, (token_block + 1) * block)
        token = token_block * block + lax.broadcasted_iota(jnp.int32, (1, block), 1)
        value = jnp.zeros((rank, block), jnp.float32) if rows[0] == 0 else v_ref[token_block]
        for row, (start, stop) in enumerate(ranges):
            inside = (token >= start) & (token < stop)
            value = jnp.where(inside, part[row * rank : (row + 1) * rank, lane], value)
        v_ref[token_block] = value
    u = u_ref[:, pl.ds(rows[0] * rank, len(rows) * rank)]
    grad = lax.dot_general(u, saved_ref[...], TN, preferred_element_type=jnp.float32)
    grad = (adapter_scale * grad).astype(out_ref.dtype)
    for row, slot in enumerate(rows):
        out_ref[slot, :, pl.ds(0, width)] = grad[row * rank : (row + 1) * rank]


def all_features_kernel(slots, group, *refs):
    refs, token_ref = refs[:-2] + refs[-1:], refs[-2]
    token_ref[...] = jnp.zeros_like(token_ref)
    for start in range(0, slots, group):
        feature_kernel(slots, range(start, min(start + group, slots)), *refs)
    saved_ref, (out_ref, v_ref) = refs[1], refs[-2:]
    width, block = saved_ref.shape[1], v_ref.shape[2]
    value = v_ref[...]
    near = value.astype(out_ref.dtype)
    out_ref[:, :, pl.ds(width, block)] = near
    rest = value - near.astype(jnp.float32)
    out_ref[:, :, pl.ds(width + block, block)] = rest.astype(out_ref.dtype)


def join_kernel(own_ref, across_ref, out_ref):
    out_ref[0], out_ref[1] = own_ref[0], across_ref[...]


def merge_kernel(mixed_ref, down_ref, v_ref):
    count = mixed_ref.shape[0]
    block = v_ref.shape[1]
    width = mixed_ref.shape[2] - 2 * block
    total = jnp.zeros(v_ref.shape, jnp.float32)
    for source in range(count):
        down_ref[:, source * width : (source + 1) * width] = mixed_ref[source, :, pl.ds(0, width)]
        for part in range(2):
            value = mixed_ref[source, :, pl.ds(width + part * block, block)]
            total = total + value.astype(jnp.float32)
    v_ref[...] = total.astype(v_ref.dtype)


def window_kernel(slots, count, meta_ref, *refs):
    row_refs, (out_ref, sem) = refs[:count], refs[count:]
    block = row_refs[0].shape[0] - ADAPTER_RANK
    wide = out_ref.shape[0] // block
    first = meta_ref[2 * slots + meta_ref[3 * slots]]
    for i in range(wide):
        target = out_ref.at[pl.ds(i * block, block)]
        pick(
            place_of(meta_ref, slots, first + i),
            row_refs,
            lambda ref: pltpu.make_async_copy(ref.at[pl.ds(0, block)], target, sem.at[i]).start(),
        )
    for i in range(wide):
        target = out_ref.at[pl.ds(i * block, block)]
        pltpu.make_async_copy(row_refs[0].at[pl.ds(0, block)], target, sem.at[i]).wait()


def up_kernel(slots, meta_ref, same_ref, other_ref, window_ref, out_ref):
    block = same_ref.shape[2]
    span = window_ref.shape[0]
    me = meta_ref[3 * slots]
    first = meta_ref[2 * slots + me]
    values = [
        by_device(meta_ref, slots, first + i, same_ref, other_ref) for i in range(span // block)
    ]
    values = jnp.concatenate(values, axis=1)
    values = jnp.where(owned(meta_ref, slots, first * block, span), values, jnp.zeros_like(values))
    product = lax.dot_general(values, window_ref[...], NN, preferred_element_type=jnp.float32)
    out_ref[...] = (adapter_scale * product).astype(out_ref.dtype)


def regroup_kernel(in_ref, out_ref):
    width = out_ref.shape[2]
    for k in range(out_ref.shape[0]):
        out_ref[k] = in_ref[:, k * width : (k + 1) * width]


def assemble_kernel(slots, orders, meta_ref, *refs):
    own_refs, other_refs = refs[: len(orders)], refs[len(orders) : 2 * len(orders)]
    out_ref, token_ref, sem = refs[-3:]
    token_ref[...] = jnp.zeros_like(token_ref)
    width = own_refs[0].shape[-1]
    copies = []
    for order, own_ref, other_ref in zip(orders, own_refs, other_refs):
        own_ref = own_ref.at[0]
        other = 2 * swapped(order, slots) + 1
        if len(other_ref.shape) == 3:
            other, other_ref = 2 * order + 1, other_ref.at[1]
        for source, ref in ((2 * order, own_ref), (other, other_ref)):
            column = pl.multiple_of(device_at(meta_ref, slots, source) * width, width)
            target = out_ref.at[:, pl.ds(column, width)]
            copies.append(pltpu.make_async_copy(ref, target, sem.at[len(copies)]))
    for copy in copies:
        copy.start()
    for copy in copies:
        copy.wait()


def local(
    output_gradient,
    saved_input,
    frozen_matrix,
    adapter_down_maps,
    adapter_up_maps,
    token_tenants,
    tenant_slot_lookup,
):
    grad_rows = output_gradient[0]
    saved_rows = saved_input[0]
    weight = frozen_matrix[0]
    down_local = adapter_down_maps[0].T
    up_local = adapter_up_maps[0].T
    slots = tenant_slot_lookup.shape[1]
    block, out_width = grad_rows.shape
    local_width = weight.shape[0]
    count = lax.axis_size("dp")
    chips = count // 2
    wide = -(-MOST // block) + 1
    me = lax.axis_index("dp").astype(jnp.int32)
    bf16, f32 = jnp.bfloat16, jnp.float32

    slot_start, slot_count = slot_ranges(token_tenants[0], tenant_slot_lookup[0])
    first = jnp.minimum(slot_start // block, count - wide)
    devices = devices_in_order(me, count)
    ids = jnp.arange(count, dtype=jnp.int32)
    places = jnp.sum(jnp.where(devices[None, :] == ids[:, None], ids[None, :], 0), axis=1)
    meta = [slot_start, slot_count, first, me[None], devices, places]
    meta = jnp.concatenate(meta).astype(jnp.int32)

    def call(kernel, name, out, operands, in_specs, out_specs, scratch_shapes=(), aliases=None, late=()):
        arrays = list(operands) + (out if isinstance(out, list) else [out])
        held = sum(v.size * v.dtype.itemsize for v in arrays)
        held += sum(
            math.prod(v.shape) * jnp.dtype(v.dtype).itemsize
            for v in scratch_shapes
            if v.memory_space == pltpu.VMEM
        )
        number = len(operands)

        def body(*refs):
            kernel(*refs[:number], *refs[number + len(late) :])

        return pl.pallas_call(
            body,
            out_shape=out,
            in_specs=list(in_specs) + [ANY] * len(late),
            out_specs=out_specs,
            scratch_shapes=scratch_shapes,
            input_output_aliases=aliases or {},
            compiler_params=pltpu.CompilerParams(vmem_limit_bytes=min(60 * MIB, 2 * held + 4 * MIB)),
            name=name,
            cost_estimate=pl.CostEstimate(flops=0, bytes_accessed=0, transcendentals=0),
        )(*operands, *map(corner, late))

    def shape(*dims, dtype=bf16):
        return jax.ShapeDtypeStruct(dims, dtype)

    token = shape(8, 128, dtype=f32)

    last = chips - 1
    rows = jnp.concatenate([grad_rows, up_local], axis=0)
    if chips == 4:
        same = [chip_partner(rows, order) for order in range(3)]
        same.append(chip_partner(same[1], 2))
    else:
        same = [chip_partner(rows, order) for order in range(chips)]
    other = [partner(same[swapped(order, count)], 1) for order in range(chips)]
    rows_in_order = [part for pair in zip(same, other) for part in pair]

    def regroup(name, value):
        pieces = shape(count, value.shape[0], local_width)
        return call(regroup_kernel, name, pieces, (value,), [VMEM], VMEM)

    down_pieces = regroup("regroup_down", down_local)
    saved_pieces = regroup("regroup_saved", saved_rows)
    down_cols = lax.all_to_all(down_pieces, "dp", split_axis=0, concat_axis=0, tiled=True)
    down_cols = down_cols.reshape(slots * ADAPTER_RANK, local_width)
    saved_cols = lax.all_to_all(
        after(saved_pieces, down_cols, same[last]), "dp", split_axis=0, concat_axis=0, tiled=True
    ).reshape(count * block, local_width)

    up_rows = call(
        functools.partial(gather_up_kernel, slots),
        "gather_up",
        shape(slots * ADAPTER_RANK, out_width),
        (meta, *rows_in_order),
        [SMEM] + [ANY] * count,
        VMEM,
        scratch_shapes=[pltpu.SemaphoreType.DMA((count,))],
    )

    below = [None] * chips
    all_u = None
    for order in range(last, -1, -1):
        fresh = all_u is None
        operands = [meta, same[order], other[order], weight, up_rows, down_cols]
        grads, all_u = call(
            functools.partial(input_kernel, slots, order),
            "input_grad",
            [shape(2, block, local_width), shape(count * block, slots * ADAPTER_RANK)],
            operands if fresh else operands + [all_u],
            [SMEM] + [VMEM] * 5 + ([] if fresh else [ANY]),
            [VMEM, ANY],
            aliases={} if fresh else {len(operands): 1},
            scratch_shapes=[
                pltpu.VMEM((2, block, slots * ADAPTER_RANK), bf16),
                pltpu.SemaphoreType.DMA((2,)),
            ],
        )
        below[order] = to_previous(grads, 0)

    group = min(slots, 8)
    mixed, made = call(
        functools.partial(all_features_kernel, slots, group),
        "feature",
        [shape(slots, ADAPTER_RANK, local_width + 2 * block), token],
        (meta, saved_cols, down_cols, all_u),
        [SMEM] + [VMEM] * 3,
        [VMEM, VMEM],
        scratch_shapes=[pltpu.VMEM((count, ADAPTER_RANK, block), f32)],
    )
    row_window = call(
        functools.partial(window_kernel, slots, count),
        "row_window",
        shape(wide * block, out_width),
        (meta, *[in_hbm(v) for v in rows_in_order]),
        [SMEM] + [ANY] * count,
        VMEM,
        scratch_shapes=[pltpu.SemaphoreType.DMA((wide,))],
        late=(made,),
    )

    arrived, crossed = [None] * chips, [None] * chips
    for order in (0, *range(3, chips)):
        piece = after(below[order], all_u) if order else below[order]
        arrived[order] = chip_partner(piece, order)
        crossed[order] = partner(arrived[order][1], 1)
    waiting = [(order, partner(below[swapped(order, count)][1], 1)) for order in (2, 1)]

    def assemble(orders, passed=None):
        operands = [meta, *[arrived[order] for order in orders], *[crossed[order] for order in orders]]
        fresh = passed is None
        return call(
            functools.partial(assemble_kernel, slots, orders),
            "assemble",
            [shape(block, count * local_width), token],
            operands if fresh else operands + [passed],
            [SMEM] + [VMEM] * (2 * len(orders)) + ([] if fresh else [HBM]),
            [HBM, VMEM],
            scratch_shapes=[pltpu.SemaphoreType.DMA((2 * len(orders),))],
            aliases={} if fresh else {len(operands): 0},
        )

    passed, _ = assemble([0, *range(3, chips)])
    mixed = lax.all_to_all(mixed, "dp", split_axis=0, concat_axis=0, tiled=True)
    down_gradient, v_block = call(
        merge_kernel,
        "merge",
        [shape(ADAPTER_RANK, count * local_width), shape(ADAPTER_RANK, block)],
        (mixed,),
        [VMEM],
        [VMEM, VMEM],
        late=(crossed[last],),
    )
    v_parts = [chip_partner(v_block, order) for order in range(chips)]
    for order, across in waiting:
        both = call(
            join_kernel,
            "join",
            shape(2, block, local_width),
            (below[order], across),
            [VMEM, VMEM],
            VMEM,
            late=(v_block,) if order == 1 else (),
        )
        both = chip_partner(both, order)
        arrived[order], crossed[order] = both, both
    passed, _ = assemble([2, 1], passed)
    v_same = jnp.stack(v_parts)
    v_other = partner(v_same, 1)
    up_gradient = call(
        functools.partial(up_kernel, slots),
        "up_grad",
        shape(ADAPTER_RANK, out_width),
        (meta, v_same, v_other, row_window),
        [SMEM] + [VMEM] * 3,
        VMEM,
    )
    return (passed[None], down_gradient.T[None], up_gradient.T[None])


def solution(mesh):
    return jax.shard_map(
        local,
        mesh=mesh,
        in_specs=(
            P("section", "dp", None),
            P("section", "dp", None),
            P("section", "dp", None),
            P("section", None, "dp"),
            P("section", None, "dp"),
            P("section", None),
            P("section", None),
        ),
        out_specs=(P("section", "dp", None), P("section", None, "dp"), P("section", None, "dp")),
        check_vma=False,
    )
```

```python
import functools
import math

import jax
import jax.numpy as jnp
from jax import lax
from jax.experimental import pallas as pl
from jax.experimental.pallas import tpu as pltpu
from jax.sharding import PartitionSpec as P

ADAPTER_RANK = 64
MOST = 256
MIB = 1024 * 1024

adapter_scale = 2.0

NT = (((1,), (1,)), ((), ()))
TN = (((0,), (0,)), ((), ()))
NN = (((1,), (0,)), ((), ()))

ANY = pl.BlockSpec(memory_space=pl.ANY)
HBM = pl.BlockSpec(memory_space=pltpu.MemorySpace.HBM)
SMEM = pl.BlockSpec(memory_space=pltpu.SMEM)
VMEM = pl.BlockSpec(memory_space=pltpu.VMEM)


def partner(value, distance):
    count = lax.axis_size("dp")
    return lax.ppermute(value, "dp", [(i, i ^ distance) for i in range(count)])


def chip_partner(value, order):
    count = lax.axis_size("dp")
    if count == 8 and order in (1, 2):
        pairs = [(i, i ^ (2 if (i + order) % 2 else 4)) for i in range(count)]
        return lax.ppermute(value, "dp", pairs)
    return partner(value, 2 * order) if order else value


def swapped(order, count):
    return 3 - order if count == 8 and order in (1, 2) else order


def devices_in_order(me, count):
    out = []
    for order in range(count // 2):
        distance = jnp.int32(2 * order)
        if count == 8 and order in (1, 2):
            distance = jnp.where((me + order) % 2 == 1, 2, 4)
        out += [me ^ distance, me ^ distance ^ 1]
    return jnp.stack(out).astype(jnp.int32)


def corner(value):
    if value.size <= 1 << 17:
        return value
    rows = min(16, value.shape[-2])
    tile = value[(0,) * (value.ndim - 2)][:rows, :128] if value.ndim > 2 else value[:rows, :128]
    return tile


def in_place_kernel(*refs):
    pass


def after(value, *others):
    operands = [value, *map(corner, others)]
    return pl.pallas_call(
        in_place_kernel,
        out_shape=jax.ShapeDtypeStruct(value.shape, value.dtype),
        in_specs=[ANY] * len(operands),
        out_specs=ANY,
        input_output_aliases={0: 0},
        name="in_order",
    )(*operands)


def in_hbm(value):
    return pltpu.with_memory_space_constraint(value, pltpu.MemorySpace.HBM)


def to_previous(value, distance):
    sections, count = lax.axis_size("section"), lax.axis_size("dp")
    pairs = [
        (s * count + i, (s - 1) * count + (i ^ distance))
        for s in range(1, sections)
        for i in range(count)
    ]
    return lax.ppermute(value, ("section", "dp"), pairs)


def slot_ranges(tenant_row, slot_table):
    tenants = slot_table.shape[0]
    ids = jnp.arange(tenants, dtype=jnp.int32)
    counts = jnp.sum((tenant_row[None, :] == ids[:, None]).astype(jnp.int32), axis=1)
    starts = jnp.sum((tenant_row[None, :] < ids[:, None]).astype(jnp.int32), axis=1)
    owner = slot_table[None, :] == ids[:, None]
    slot_start = jnp.sum(jnp.where(owner, starts[None, :], 0), axis=1)
    slot_count = jnp.sum(jnp.where(owner, counts[None, :], 0), axis=1)
    return slot_start, slot_count


def pick(index, refs, act):
    for k, ref in enumerate(refs):

        @pl.when(index == k)
        def _():
            act(ref)


def device_at(meta_ref, slots, place):
    return meta_ref[3 * slots + 1 + place]


def place_of(meta_ref, slots, device):
    return meta_ref[4 * slots + 1 + device]


def owned(meta_ref, slots, first_token, width):
    me = meta_ref[3 * slots]
    start, count = meta_ref[me], meta_ref[slots + me]
    token = first_token + lax.broadcasted_iota(jnp.int32, (1, width), 1)
    return (token >= start) & (token < start + count)


def slot_lanes(meta_ref, slots, rank):
    lane = lax.broadcasted_iota(jnp.int32, (1, slots * rank), 1)
    start = jnp.zeros_like(lane)
    stop = jnp.zeros_like(lane)
    for slot in range(slots):
        first = meta_ref[slot]
        inside = lane >= slot * rank
        start = jnp.where(inside, first, start)
        stop = jnp.where(inside, first + meta_ref[slots + slot], stop)
    return start, stop


class Loads:
    def __init__(self, sem):
        self.sem, self.copies = sem, {}

    def start(self, name, source, target):
        copy = pltpu.make_async_copy(source, target, self.sem.at[len(self.copies)])
        copy.start()
        self.copies[name] = copy

    def wait(self, *names):
        for name in names:
            self.copies[name].wait()


def load_input(loads, weight_ref, down_ref, weight, down):
    half = weight_ref.shape[0] // 2
    loads.start("down", down_ref, down)
    for i in range(2):
        span = pl.ds(i * half, half)
        loads.start(("weight", i), weight_ref.at[span], weight.at[span])


def write_input(loads, arriving, rows, ranks, weight, down, out_ref):
    block = out_ref.shape[1]
    half = weight.shape[0] // 2
    if arriving:
        loads.wait("down")
    for i in range(2):
        span = pl.ds(i * half, half)
        term = lax.dot_general(ranks, down[:, span], NN, preferred_element_type=jnp.float32)
        if arriving:
            loads.wait(("weight", i))
        total = lax.dot_general(rows, weight[span, :], NT, preferred_element_type=jnp.float32)
        total = (total + adapter_scale * term).astype(out_ref.dtype)
        out_ref[0, :, span], out_ref[1, :, span] = total[:block], total[block:]


def write_ranks(meta_ref, slots, order, u, lanes, held, all_u_ref, stores):
    block = held.shape[1]
    start, stop = lanes
    token = lax.broadcasted_iota(jnp.int32, (block, 1), 0)
    parts = []
    for core in range(2):
        row = pl.multiple_of(device_at(meta_ref, slots, 2 * order + core) * block, block)
        inside = (token + row >= start) & (token + row < stop)
        part = jnp.where(inside, u[core * block : (core + 1) * block], 0.0).astype(held.dtype)
        held[core] = part
        stores.start((order, core), held.at[core], all_u_ref.at[pl.ds(row, block)])
        parts.append(part)
    return jnp.concatenate(parts, axis=0)


def first_input_kernel(slots, order, meta_ref, *refs):
    row_refs, (weight_ref, down_ref, out_ref, all_u_ref, up), refs = (
        refs[:slots],
        refs[slots : slots + 5],
        refs[slots + 5 :],
    )
    rows, weight, down, held, sem, u_sem = refs
    block = out_ref.shape[1]
    rank = up.shape[0] // slots
    loads, stores = Loads(sem), Loads(u_sem)
    for k, ref in enumerate(row_refs):
        row = pl.multiple_of(device_at(meta_ref, slots, k) * rank, rank)
        loads.start(("up", k), ref.at[pl.ds(block, rank)], up.at[pl.ds(row, rank)])
    for core in range(2):
        source = row_refs[2 * order + core].at[pl.ds(0, block)]
        loads.start(("rows", core), source, rows.at[pl.ds(core * block, block)])
    load_input(loads, weight_ref, down_ref, weight, down)
    lanes = slot_lanes(meta_ref, slots, rank)
    loads.wait(*[("up", k) for k in range(slots)], ("rows", 0), ("rows", 1))
    u = lax.dot_general(rows[...], up[...], NT, preferred_element_type=jnp.float32)
    ranks = write_ranks(meta_ref, slots, order, u, lanes, held, all_u_ref, stores)
    write_input(loads, True, rows[...], ranks, weight, down, out_ref)
    stores.wait((order, 0), (order, 1))


def later_input_kernel(slots, orders, meta_ref, weight_ref, down_ref, up_ref, *refs):
    number = len(orders)
    row_refs, out_refs = refs[: 2 * number], refs[2 * number + 1 : 3 * number + 1]
    all_u_ref, held, u_sem = refs[3 * number + 1 :]
    block = out_refs[0].shape[1]
    stores = Loads(u_sem)
    lanes = slot_lanes(meta_ref, slots, up_ref.shape[0] // slots)
    for i, order in enumerate(orders):
        rows = [ref[pl.ds(0, block)] for ref in row_refs[2 * i : 2 * i + 2]]
        rows = jnp.concatenate(rows, axis=0)
        u = lax.dot_general(rows, up_ref[...], NT, preferred_element_type=jnp.float32)
        span = pl.ds(2 * i, 2)
        ranks = write_ranks(meta_ref, slots, order, u, lanes, held.at[span], all_u_ref, stores)
        write_input(None, False, rows, ranks, weight_ref, down_ref, out_refs[i])
    stores.wait(*stores.copies)


def feature_kernel(slots, rows, meta_ref, saved_ref, down_ref, u_ref, out_ref, v_ref):
    rank, block = v_ref.shape[1:]
    width = saved_ref.shape[1]
    blocks = v_ref.shape[0]
    down = down_ref[pl.ds(rows[0] * rank, len(rows) * rank), :]
    part = lax.dot_general(down, saved_ref[...], NT, preferred_element_type=jnp.float32)
    ranges = []
    for slot in rows:
        ranges.append((meta_ref[slot], meta_ref[slot] + meta_ref[slots + slot]))
    for token_block in range(blocks):
        lane = slice(token_block * block, (token_block + 1) * block)
        token = token_block * block + lax.broadcasted_iota(jnp.int32, (1, block), 1)
        value = jnp.zeros((rank, block), jnp.float32) if rows[0] == 0 else v_ref[token_block]
        for row, (start, stop) in enumerate(ranges):
            inside = (token >= start) & (token < stop)
            value = jnp.where(inside, part[row * rank : (row + 1) * rank, lane], value)
        v_ref[token_block] = value
    u = u_ref[:, pl.ds(rows[0] * rank, len(rows) * rank)]
    grad = lax.dot_general(u, saved_ref[...], TN, preferred_element_type=jnp.float32)
    grad = (adapter_scale * grad).astype(out_ref.dtype)
    for row, slot in enumerate(rows):
        out_ref[slot, :, pl.ds(0, width)] = grad[row * rank : (row + 1) * rank]


def all_features_kernel(slots, group, *refs):
    refs, token_ref = refs[:-2] + refs[-1:], refs[-2]
    token_ref[...] = jnp.zeros_like(token_ref)
    for start in range(0, slots, group):
        feature_kernel(slots, range(start, min(start + group, slots)), *refs)
    saved_ref, (out_ref, v_ref) = refs[1], refs[-2:]
    width, block = saved_ref.shape[1], v_ref.shape[2]
    value = v_ref[...]
    near = value.astype(out_ref.dtype)
    out_ref[:, :, pl.ds(width, block)] = near
    rest = value - near.astype(jnp.float32)
    out_ref[:, :, pl.ds(width + block, block)] = rest.astype(out_ref.dtype)


def join_kernel(own_ref, across_ref, out_ref):
    out_ref[0], out_ref[1] = own_ref[0], across_ref[...]


def merge_kernel(mixed_ref, down_ref, v_ref):
    count = mixed_ref.shape[0]
    block = v_ref.shape[2]
    width = mixed_ref.shape[2] - 2 * block
    total = jnp.zeros(v_ref.shape[1:], jnp.float32)
    for source in range(count):
        down_ref[:, source * width : (source + 1) * width] = mixed_ref[source, :, pl.ds(0, width)]
        for part in range(2):
            value = mixed_ref[source, :, pl.ds(width + part * block, block)]
            total = total + value.astype(jnp.float32)
    total = total.astype(v_ref.dtype)
    for target in range(count):
        v_ref[target] = total


def window_kernel(slots, count, meta_ref, *refs):
    row_refs, (out_ref, sem) = refs[:count], refs[count:]
    block = row_refs[0].shape[0] - ADAPTER_RANK
    wide = out_ref.shape[0] // block
    first = meta_ref[2 * slots + meta_ref[3 * slots]]
    for i in range(wide):
        target = out_ref.at[pl.ds(i * block, block)]
        pick(
            place_of(meta_ref, slots, first + i),
            row_refs,
            lambda ref: pltpu.make_async_copy(ref.at[pl.ds(0, block)], target, sem.at[i]).start(),
        )
    for i in range(wide):
        target = out_ref.at[pl.ds(i * block, block)]
        pltpu.make_async_copy(row_refs[0].at[pl.ds(0, block)], target, sem.at[i]).wait()


def up_kernel(slots, meta_ref, v_ref, window_ref, out_ref):
    block = v_ref.shape[2]
    span = window_ref.shape[0]
    me = meta_ref[3 * slots]
    first = meta_ref[2 * slots + me]
    values = [v_ref[first + i] for i in range(span // block)]
    values = jnp.concatenate(values, axis=1)
    values = jnp.where(owned(meta_ref, slots, first * block, span), values, jnp.zeros_like(values))
    product = lax.dot_general(values, window_ref[...], NN, preferred_element_type=jnp.float32)
    out_ref[...] = (adapter_scale * product).astype(out_ref.dtype)


def regroup_kernel(in_ref, out_ref):
    width = out_ref.shape[2]
    for k in range(out_ref.shape[0]):
        out_ref[k] = in_ref[:, k * width : (k + 1) * width]


def assemble_kernel(slots, orders, meta_ref, *refs):
    own_refs, other_refs = refs[: len(orders)], refs[len(orders) : 2 * len(orders)]
    out_ref, token_ref, sem = refs[-3:]
    token_ref[...] = jnp.zeros_like(token_ref)
    width = own_refs[0].shape[-1]
    copies = []
    for order, own_ref, other_ref in zip(orders, own_refs, other_refs):
        own_ref = own_ref.at[0]
        other = 2 * swapped(order, slots) + 1
        if len(other_ref.shape) == 3:
            other, other_ref = 2 * order + 1, other_ref.at[1]
        for source, ref in ((2 * order, own_ref), (other, other_ref)):
            column = pl.multiple_of(device_at(meta_ref, slots, source) * width, width)
            target = out_ref.at[:, pl.ds(column, width)]
            copies.append(pltpu.make_async_copy(ref, target, sem.at[len(copies)]))
    for copy in copies:
        copy.start()
    for copy in copies:
        copy.wait()


def local(
    output_gradient,
    saved_input,
    frozen_matrix,
    adapter_down_maps,
    adapter_up_maps,
    token_tenants,
    tenant_slot_lookup,
):
    grad_rows = output_gradient[0]
    saved_rows = saved_input[0]
    weight = frozen_matrix[0]
    down_local = adapter_down_maps[0].T
    up_local = adapter_up_maps[0].T
    slots = tenant_slot_lookup.shape[1]
    block, out_width = grad_rows.shape
    local_width = weight.shape[0]
    count = lax.axis_size("dp")
    chips = count // 2
    wide = -(-MOST // block) + 1
    me = lax.axis_index("dp").astype(jnp.int32)
    bf16, f32 = jnp.bfloat16, jnp.float32

    slot_start, slot_count = slot_ranges(token_tenants[0], tenant_slot_lookup[0])
    first = jnp.minimum(slot_start // block, count - wide)
    devices = devices_in_order(me, count)
    ids = jnp.arange(count, dtype=jnp.int32)
    places = jnp.sum(jnp.where(devices[None, :] == ids[:, None], ids[None, :], 0), axis=1)
    meta = [slot_start, slot_count, first, me[None], devices, places]
    meta = jnp.concatenate(meta).astype(jnp.int32)

    def call(kernel, name, out, operands, in_specs, out_specs, scratch_shapes=(), aliases=None, late=()):
        arrays = list(operands) + (out if isinstance(out, list) else [out])
        held = sum(v.size * v.dtype.itemsize for v in arrays)
        held += sum(
            math.prod(v.shape) * jnp.dtype(v.dtype).itemsize
            for v in scratch_shapes
            if v.memory_space == pltpu.VMEM
        )
        number = len(operands)

        def body(*refs):
            kernel(*refs[:number], *refs[number + len(late) :])

        return pl.pallas_call(
            body,
            out_shape=out,
            in_specs=list(in_specs) + [ANY] * len(late),
            out_specs=out_specs,
            scratch_shapes=scratch_shapes,
            input_output_aliases=aliases or {},
            compiler_params=pltpu.CompilerParams(vmem_limit_bytes=min(60 * MIB, 2 * held + 4 * MIB)),
            name=name,
            cost_estimate=pl.CostEstimate(flops=0, bytes_accessed=0, transcendentals=0),
        )(*operands, *map(corner, late))

    def shape(*dims, dtype=bf16):
        return jax.ShapeDtypeStruct(dims, dtype)

    token = shape(8, 128, dtype=f32)

    last = chips - 1
    rows = jnp.concatenate([grad_rows, up_local], axis=0)
    if chips == 4:
        same = [chip_partner(rows, order) for order in range(3)]
        same.append(chip_partner(same[1], 2))
    else:
        same = [chip_partner(rows, order) for order in range(chips)]
    other = [partner(same[swapped(order, count)], 1) for order in range(chips)]
    rows_in_order = [part for pair in zip(same, other) for part in pair]

    def regroup(name, value):
        pieces = shape(count, value.shape[0], local_width)
        return call(regroup_kernel, name, pieces, (value,), [VMEM], VMEM)

    down_pieces = regroup("regroup_down", down_local)
    saved_pieces = regroup("regroup_saved", saved_rows)
    down_cols = lax.all_to_all(down_pieces, "dp", split_axis=0, concat_axis=0, tiled=True)
    down_cols = down_cols.reshape(slots * ADAPTER_RANK, local_width)
    saved_cols = lax.all_to_all(
        after(saved_pieces, down_cols, same[last]), "dp", split_axis=0, concat_axis=0, tiled=True
    ).reshape(count * block, local_width)

    below = [None] * chips
    hbm_operands = [in_hbm(v) for v in (*rows_in_order, weight, down_cols)]
    all_u_shape = shape(count * block, slots * ADAPTER_RANK)
    piece = shape(2, block, local_width)
    grads, all_u, up_rows = call(
        functools.partial(first_input_kernel, slots, last),
        "first_input",
        [piece, all_u_shape, shape(slots * ADAPTER_RANK, out_width)],
        (meta, *hbm_operands),
        [SMEM] + [ANY] * len(hbm_operands),
        [VMEM, ANY, VMEM],
        scratch_shapes=[
            pltpu.VMEM((2 * block, out_width), bf16),
            pltpu.VMEM(weight.shape, bf16),
            pltpu.VMEM(down_cols.shape, bf16),
            pltpu.VMEM((2, block, slots * ADAPTER_RANK), bf16),
            pltpu.SemaphoreType.DMA((slots + 5,)),
            pltpu.SemaphoreType.DMA((2,)),
        ],
    )
    below[last] = to_previous(grads, 0)
    for top in range(last - 1, -1, -3):
        orders = range(top, max(top - 3, -1), -1)
        row_parts = [part for order in orders for part in (same[order], other[order])]
        operands = (meta, weight, down_cols, up_rows, *row_parts, all_u)
        *grads, all_u = call(
            functools.partial(later_input_kernel, slots, orders),
            "later_input",
            [piece] * len(orders) + [all_u_shape],
            operands,
            [SMEM] + [VMEM] * (3 + len(row_parts)) + [ANY],
            [VMEM] * len(orders) + [ANY],
            aliases={len(operands) - 1: len(orders)},
            scratch_shapes=[
                pltpu.VMEM((2 * len(orders), block, slots * ADAPTER_RANK), bf16),
                pltpu.SemaphoreType.DMA((2 * len(orders),)),
            ],
        )
        for order, value in zip(orders, grads):
            below[order] = to_previous(value, 0)

    group = min(slots, 8)
    mixed, made = call(
        functools.partial(all_features_kernel, slots, group),
        "feature",
        [shape(slots, ADAPTER_RANK, local_width + 2 * block), token],
        (meta, saved_cols, down_cols, all_u),
        [SMEM] + [VMEM] * 3,
        [VMEM, VMEM],
        scratch_shapes=[pltpu.VMEM((count, ADAPTER_RANK, block), f32)],
    )
    row_window = call(
        functools.partial(window_kernel, slots, count),
        "row_window",
        shape(wide * block, out_width),
        (meta, *[in_hbm(v) for v in rows_in_order]),
        [SMEM] + [ANY] * count,
        VMEM,
        scratch_shapes=[pltpu.SemaphoreType.DMA((wide,))],
        late=(made,),
    )

    arrived, crossed = [None] * chips, [None] * chips
    for order in (0, *range(3, chips)):
        piece = below[order]
        arrived[order] = chip_partner(piece, order)
        crossed[order] = partner(arrived[order][1], 1)
    waiting = [(order, partner(below[swapped(order, count)][1], 1)) for order in (2, 1)]

    def assemble(orders, passed=None):
        operands = [meta, *[arrived[order] for order in orders], *[crossed[order] for order in orders]]
        fresh = passed is None
        return call(
            functools.partial(assemble_kernel, slots, orders),
            "assemble",
            [shape(block, count * local_width), token],
            operands if fresh else operands + [passed],
            [SMEM] + [VMEM] * (2 * len(orders)) + ([] if fresh else [HBM]),
            [HBM, VMEM],
            scratch_shapes=[pltpu.SemaphoreType.DMA((2 * len(orders),))],
            aliases={} if fresh else {len(operands): 0},
        )

    passed, _ = assemble([0, *range(3, chips)])
    mixed = lax.all_to_all(mixed, "dp", split_axis=0, concat_axis=0, tiled=True)
    down_gradient, v_block = call(
        merge_kernel,
        "merge",
        [shape(ADAPTER_RANK, count * local_width), shape(count, ADAPTER_RANK, block)],
        (mixed,),
        [VMEM],
        [VMEM, VMEM],
        late=(crossed[last], row_window),
    )
    v_all = lax.all_to_all(v_block, "dp", split_axis=0, concat_axis=0, tiled=True)
    for order, across in waiting:
        both = call(
            join_kernel,
            "join",
            shape(2, block, local_width),
            (below[order], across),
            [VMEM, VMEM],
            VMEM,
            late=(v_block,) if order == 1 else (),
        )
        both = chip_partner(both, order)
        arrived[order], crossed[order] = both, both
    passed, _ = assemble([2, 1], passed)
    up_gradient = call(
        functools.partial(up_kernel, slots),
        "up_grad",
        shape(ADAPTER_RANK, out_width),
        (meta, v_all, row_window),
        [SMEM] + [VMEM] * 2,
        VMEM,
    )
    return (passed[None], down_gradient.T[None], up_gradient.T[None])


def solution(mesh):
    return jax.shard_map(
        local,
        mesh=mesh,
        in_specs=(
            P("section", "dp", None),
            P("section", "dp", None),
            P("section", "dp", None),
            P("section", None, "dp"),
            P("section", None, "dp"),
            P("section", None),
            P("section", None),
        ),
        out_specs=(P("section", "dp", None), P("section", None, "dp"), P("section", None, "dp")),
        check_vma=False,
    )
```

```python
import functools
import math

import jax
import jax.numpy as jnp
from jax import lax
from jax.experimental import pallas as pl
from jax.experimental.pallas import tpu as pltpu
from jax.sharding import PartitionSpec as P

ADAPTER_RANK = 64
MOST = 256
MIB = 1024 * 1024

adapter_scale = 2.0

NT = (((1,), (1,)), ((), ()))
TN = (((0,), (0,)), ((), ()))
NN = (((1,), (0,)), ((), ()))

ANY = pl.BlockSpec(memory_space=pl.ANY)
HBM = pl.BlockSpec(memory_space=pltpu.MemorySpace.HBM)
SMEM = pl.BlockSpec(memory_space=pltpu.SMEM)
VMEM = pl.BlockSpec(memory_space=pltpu.VMEM)


def partner(value, distance):
    count = lax.axis_size("dp")
    return lax.ppermute(value, "dp", [(i, i ^ distance) for i in range(count)])


def chip_partner(value, order):
    count = lax.axis_size("dp")
    if count == 8 and order in (1, 2):
        pairs = [(i, i ^ (2 if (i + order) % 2 else 4)) for i in range(count)]
        return lax.ppermute(value, "dp", pairs)
    return partner(value, 2 * order) if order else value


def swapped(order, count):
    return 3 - order if count == 8 and order in (1, 2) else order


def devices_in_order(me, count):
    out = []
    for order in range(count // 2):
        distance = jnp.int32(2 * order)
        if count == 8 and order in (1, 2):
            distance = jnp.where((me + order) % 2 == 1, 2, 4)
        out += [me ^ distance, me ^ distance ^ 1]
    return jnp.stack(out).astype(jnp.int32)


def corner(value):
    if value.size <= 1 << 17:
        return value
    rows = min(16, value.shape[-2])
    tile = value[(0,) * (value.ndim - 2)][:rows, :128] if value.ndim > 2 else value[:rows, :128]
    return tile


def in_place_kernel(*refs):
    pass


def after(value, *others):
    operands = [value, *map(corner, others)]
    return pl.pallas_call(
        in_place_kernel,
        out_shape=jax.ShapeDtypeStruct(value.shape, value.dtype),
        in_specs=[ANY] * len(operands),
        out_specs=ANY,
        input_output_aliases={0: 0},
        name="in_order",
    )(*operands)


def in_hbm(value):
    return pltpu.with_memory_space_constraint(value, pltpu.MemorySpace.HBM)


def to_previous(value, distance):
    sections, count = lax.axis_size("section"), lax.axis_size("dp")
    pairs = [
        (s * count + i, (s - 1) * count + (i ^ distance))
        for s in range(1, sections)
        for i in range(count)
    ]
    return lax.ppermute(value, ("section", "dp"), pairs)


def slot_ranges(tenant_row, slot_table):
    tenants = slot_table.shape[0]
    ids = jnp.arange(tenants, dtype=jnp.int32)
    counts = jnp.sum((tenant_row[None, :] == ids[:, None]).astype(jnp.int32), axis=1)
    starts = jnp.sum((tenant_row[None, :] < ids[:, None]).astype(jnp.int32), axis=1)
    owner = slot_table[None, :] == ids[:, None]
    slot_start = jnp.sum(jnp.where(owner, starts[None, :], 0), axis=1)
    slot_count = jnp.sum(jnp.where(owner, counts[None, :], 0), axis=1)
    return slot_start, slot_count


def pick(index, refs, act):
    for k, ref in enumerate(refs):

        @pl.when(index == k)
        def _():
            act(ref)


def device_at(meta_ref, slots, place):
    return meta_ref[3 * slots + 1 + place]


def place_of(meta_ref, slots, device):
    return meta_ref[4 * slots + 1 + device]


def owned(meta_ref, slots, first_token, width):
    me = meta_ref[3 * slots]
    start, count = meta_ref[me], meta_ref[slots + me]
    token = first_token + lax.broadcasted_iota(jnp.int32, (1, width), 1)
    return (token >= start) & (token < start + count)


def slot_lanes(meta_ref, slots, rank):
    lane = lax.broadcasted_iota(jnp.int32, (1, slots * rank), 1)
    start = jnp.zeros_like(lane)
    stop = jnp.zeros_like(lane)
    for slot in range(slots):
        first = meta_ref[slot]
        inside = lane >= slot * rank
        start = jnp.where(inside, first, start)
        stop = jnp.where(inside, first + meta_ref[slots + slot], stop)
    return start, stop


class Loads:
    def __init__(self, sem):
        self.sem, self.copies = sem, {}

    def start(self, name, source, target):
        copy = pltpu.make_async_copy(source, target, self.sem.at[len(self.copies)])
        copy.start()
        self.copies[name] = copy

    def wait(self, *names):
        for name in names:
            self.copies[name].wait()


def load_input(loads, weight_ref, down_ref, weight, down):
    half = weight_ref.shape[0] // 2
    loads.start("down", down_ref, down)
    for i in range(2):
        span = pl.ds(i * half, half)
        loads.start(("weight", i), weight_ref.at[span], weight.at[span])


def write_input(loads, arriving, rows, ranks, weight, down, out_ref):
    block = out_ref.shape[1]
    half = weight.shape[0] // 2
    if arriving:
        loads.wait("down")
    for i in range(2):
        span = pl.ds(i * half, half)
        term = lax.dot_general(ranks, down[:, span], NN, preferred_element_type=jnp.float32)
        if arriving:
            loads.wait(("weight", i))
        total = lax.dot_general(rows, weight[span, :], NT, preferred_element_type=jnp.float32)
        total = (total + adapter_scale * term).astype(out_ref.dtype)
        out_ref[0, :, span], out_ref[1, :, span] = total[:block], total[block:]


def write_ranks(meta_ref, slots, order, u, lanes, held, all_u_ref, stores):
    block = held.shape[1]
    start, stop = lanes
    token = lax.broadcasted_iota(jnp.int32, (block, 1), 0)
    parts = []
    for core in range(2):
        row = pl.multiple_of(device_at(meta_ref, slots, 2 * order + core) * block, block)
        inside = (token + row >= start) & (token + row < stop)
        part = jnp.where(inside, u[core * block : (core + 1) * block], 0.0).astype(held.dtype)
        held[core] = part
        stores.start((order, core), held.at[core], all_u_ref.at[pl.ds(row, block)])
        parts.append(part)
    return jnp.concatenate(parts, axis=0)


def first_input_kernel(slots, order, meta_ref, *refs):
    row_refs, (weight_ref, down_ref, out_ref, all_u_ref, up), refs = (
        refs[:slots],
        refs[slots : slots + 5],
        refs[slots + 5 :],
    )
    rows, weight, down, held, sem, u_sem = refs
    block = out_ref.shape[1]
    rank = up.shape[0] // slots
    loads, stores = Loads(sem), Loads(u_sem)
    for k, ref in enumerate(row_refs):
        row = pl.multiple_of(device_at(meta_ref, slots, k) * rank, rank)
        loads.start(("up", k), ref.at[pl.ds(block, rank)], up.at[pl.ds(row, rank)])
    for core in range(2):
        source = row_refs[2 * order + core].at[pl.ds(0, block)]
        loads.start(("rows", core), source, rows.at[pl.ds(core * block, block)])
    load_input(loads, weight_ref, down_ref, weight, down)
    lanes = slot_lanes(meta_ref, slots, rank)
    loads.wait(*[("up", k) for k in range(slots)], ("rows", 0), ("rows", 1))
    u = lax.dot_general(rows[...], up[...], NT, preferred_element_type=jnp.float32)
    ranks = write_ranks(meta_ref, slots, order, u, lanes, held, all_u_ref, stores)
    write_input(loads, True, rows[...], ranks, weight, down, out_ref)
    stores.wait((order, 0), (order, 1))


def later_input_kernel(slots, orders, meta_ref, weight_ref, down_ref, up_ref, *refs):
    number = len(orders)
    row_refs, out_refs = refs[: 2 * number], refs[2 * number + 1 : 3 * number + 1]
    all_u_ref, held, u_sem = refs[3 * number + 1 :]
    block = out_refs[0].shape[1]
    stores = Loads(u_sem)
    lanes = slot_lanes(meta_ref, slots, up_ref.shape[0] // slots)
    for i, order in enumerate(orders):
        rows = [ref[pl.ds(0, block)] for ref in row_refs[2 * i : 2 * i + 2]]
        rows = jnp.concatenate(rows, axis=0)
        u = lax.dot_general(rows, up_ref[...], NT, preferred_element_type=jnp.float32)
        span = pl.ds(2 * i, 2)
        ranks = write_ranks(meta_ref, slots, order, u, lanes, held.at[span], all_u_ref, stores)
        write_input(None, False, rows, ranks, weight_ref, down_ref, out_refs[i])
    stores.wait(*stores.copies)


def feature_kernel(slots, rows, meta_ref, saved_ref, down_ref, u_ref, out_ref, v_ref):
    rank, block = v_ref.shape[1:]
    width = saved_ref.shape[1]
    blocks = v_ref.shape[0]
    down = down_ref[pl.ds(rows[0] * rank, len(rows) * rank), :]
    part = lax.dot_general(down, saved_ref[...], NT, preferred_element_type=jnp.float32)
    ranges = []
    for slot in rows:
        ranges.append((meta_ref[slot], meta_ref[slot] + meta_ref[slots + slot]))
    for token_block in range(blocks):
        lane = slice(token_block * block, (token_block + 1) * block)
        token = token_block * block + lax.broadcasted_iota(jnp.int32, (1, block), 1)
        value = jnp.zeros((rank, block), jnp.float32) if rows[0] == 0 else v_ref[token_block]
        for row, (start, stop) in enumerate(ranges):
            inside = (token >= start) & (token < stop)
            value = jnp.where(inside, part[row * rank : (row + 1) * rank, lane], value)
        v_ref[token_block] = value
    u = u_ref[:, pl.ds(rows[0] * rank, len(rows) * rank)]
    grad = lax.dot_general(u, saved_ref[...], TN, preferred_element_type=jnp.float32)
    grad = (adapter_scale * grad).astype(out_ref.dtype)
    for row, slot in enumerate(rows):
        out_ref[slot, :, pl.ds(0, width)] = grad[row * rank : (row + 1) * rank]


def all_features_kernel(slots, group, *refs):
    refs, token_ref = refs[:-2] + refs[-1:], refs[-2]
    token_ref[...] = jnp.zeros_like(token_ref)
    for start in range(0, slots, group):
        feature_kernel(slots, range(start, min(start + group, slots)), *refs)
    saved_ref, (out_ref, v_ref) = refs[1], refs[-2:]
    width, block = saved_ref.shape[1], v_ref.shape[2]
    value = v_ref[...]
    near = value.astype(out_ref.dtype)
    out_ref[:, :, pl.ds(width, block)] = near
    rest = value - near.astype(jnp.float32)
    out_ref[:, :, pl.ds(width + block, block)] = rest.astype(out_ref.dtype)


def join_kernel(own_ref, across_ref, out_ref):
    out_ref[0], out_ref[1] = own_ref[0], across_ref[...]


def merge_kernel(mixed_ref, down_ref, v_ref):
    count = mixed_ref.shape[0]
    block = v_ref.shape[2]
    width = mixed_ref.shape[2] - 2 * block
    total = jnp.zeros(v_ref.shape[1:], jnp.float32)
    for source in range(count):
        down_ref[:, source * width : (source + 1) * width] = mixed_ref[source, :, pl.ds(0, width)]
        for part in range(2):
            value = mixed_ref[source, :, pl.ds(width + part * block, block)]
            total = total + value.astype(jnp.float32)
    total = total.astype(v_ref.dtype)
    for target in range(count):
        v_ref[target] = total


def window_kernel(slots, count, meta_ref, *refs):
    row_refs, (out_ref, sem) = refs[:count], refs[count:]
    block = row_refs[0].shape[0] - ADAPTER_RANK
    wide = out_ref.shape[0] // block
    first = meta_ref[2 * slots + meta_ref[3 * slots]]
    for i in range(wide):
        target = out_ref.at[pl.ds(i * block, block)]
        pick(
            place_of(meta_ref, slots, first + i),
            row_refs,
            lambda ref: pltpu.make_async_copy(ref.at[pl.ds(0, block)], target, sem.at[i]).start(),
        )
    for i in range(wide):
        target = out_ref.at[pl.ds(i * block, block)]
        pltpu.make_async_copy(row_refs[0].at[pl.ds(0, block)], target, sem.at[i]).wait()


def up_kernel(slots, meta_ref, v_ref, window_ref, out_ref):
    block = v_ref.shape[2]
    span = window_ref.shape[0]
    me = meta_ref[3 * slots]
    first = meta_ref[2 * slots + me]
    values = [v_ref[first + i] for i in range(span // block)]
    values = jnp.concatenate(values, axis=1)
    values = jnp.where(owned(meta_ref, slots, first * block, span), values, jnp.zeros_like(values))
    product = lax.dot_general(values, window_ref[...], NN, preferred_element_type=jnp.float32)
    out_ref[...] = (adapter_scale * product).astype(out_ref.dtype)


def regroup_kernel(in_ref, out_ref):
    width = out_ref.shape[2]
    for k in range(out_ref.shape[0]):
        out_ref[k] = in_ref[:, k * width : (k + 1) * width]


def assemble_kernel(slots, orders, meta_ref, *refs):
    own_refs, other_refs = refs[: len(orders)], refs[len(orders) : 2 * len(orders)]
    out_ref, token_ref, sem = refs[-3:]
    token_ref[...] = jnp.zeros_like(token_ref)
    width = own_refs[0].shape[-1]
    copies = []
    for order, own_ref, other_ref in zip(orders, own_refs, other_refs):
        own_ref = own_ref.at[0]
        other = 2 * swapped(order, slots) + 1
        if len(other_ref.shape) == 3:
            other, other_ref = 2 * order + 1, other_ref.at[1]
        for source, ref in ((2 * order, own_ref), (other, other_ref)):
            column = pl.multiple_of(device_at(meta_ref, slots, source) * width, width)
            target = out_ref.at[:, pl.ds(column, width)]
            copies.append(pltpu.make_async_copy(ref, target, sem.at[len(copies)]))
    for copy in copies:
        copy.start()
    for copy in copies:
        copy.wait()


def local(
    output_gradient,
    saved_input,
    frozen_matrix,
    adapter_down_maps,
    adapter_up_maps,
    token_tenants,
    tenant_slot_lookup,
):
    grad_rows = output_gradient[0]
    saved_rows = saved_input[0]
    weight = frozen_matrix[0]
    down_local = adapter_down_maps[0].T
    up_local = adapter_up_maps[0].T
    slots = tenant_slot_lookup.shape[1]
    block, out_width = grad_rows.shape
    local_width = weight.shape[0]
    count = lax.axis_size("dp")
    chips = count // 2
    wide = -(-MOST // block) + 1
    me = lax.axis_index("dp").astype(jnp.int32)
    bf16, f32 = jnp.bfloat16, jnp.float32

    slot_start, slot_count = slot_ranges(token_tenants[0], tenant_slot_lookup[0])
    first = jnp.minimum(slot_start // block, count - wide)
    devices = devices_in_order(me, count)
    ids = jnp.arange(count, dtype=jnp.int32)
    places = jnp.sum(jnp.where(devices[None, :] == ids[:, None], ids[None, :], 0), axis=1)
    meta = [slot_start, slot_count, first, me[None], devices, places]
    meta = jnp.concatenate(meta).astype(jnp.int32)

    def call(kernel, name, out, operands, in_specs, out_specs, scratch_shapes=(), aliases=None, late=()):
        arrays = list(operands) + (out if isinstance(out, list) else [out])
        held = sum(v.size * v.dtype.itemsize for v in arrays)
        held += sum(
            math.prod(v.shape) * jnp.dtype(v.dtype).itemsize
            for v in scratch_shapes
            if v.memory_space == pltpu.VMEM
        )
        number = len(operands)

        def body(*refs):
            kernel(*refs[:number], *refs[number + len(late) :])

        return pl.pallas_call(
            body,
            out_shape=out,
            in_specs=list(in_specs) + [ANY] * len(late),
            out_specs=out_specs,
            scratch_shapes=scratch_shapes,
            input_output_aliases=aliases or {},
            compiler_params=pltpu.CompilerParams(vmem_limit_bytes=min(60 * MIB, 2 * held + 4 * MIB)),
            name=name,
            cost_estimate=pl.CostEstimate(flops=0, bytes_accessed=0, transcendentals=0),
        )(*operands, *map(corner, late))

    def shape(*dims, dtype=bf16):
        return jax.ShapeDtypeStruct(dims, dtype)

    token = shape(8, 128, dtype=f32)

    last = chips - 1
    rows = jnp.concatenate([grad_rows, up_local], axis=0)
    if chips == 4:
        same = [chip_partner(rows, order) for order in range(3)]
        same.append(chip_partner(same[1], 2))
    else:
        same = [chip_partner(rows, order) for order in range(chips)]
    other = [partner(same[swapped(order, count)], 1) for order in range(chips)]
    rows_in_order = [part for pair in zip(same, other) for part in pair]

    def regroup(name, value):
        pieces = shape(count, value.shape[0], local_width)
        return call(regroup_kernel, name, pieces, (value,), [VMEM], VMEM)

    down_pieces = regroup("regroup_down", down_local)
    saved_pieces = regroup("regroup_saved", saved_rows)
    down_cols = lax.all_to_all(down_pieces, "dp", split_axis=0, concat_axis=0, tiled=True)
    down_cols = down_cols.reshape(slots * ADAPTER_RANK, local_width)
    saved_cols = lax.all_to_all(
        after(saved_pieces, down_cols, same[last]), "dp", split_axis=0, concat_axis=0, tiled=True
    ).reshape(count * block, local_width)

    below = [None] * chips
    hbm_operands = [in_hbm(v) for v in (*rows_in_order, weight, down_cols)]
    all_u_shape = shape(count * block, slots * ADAPTER_RANK)
    piece = shape(2, block, local_width)
    grads, all_u, up_rows = call(
        functools.partial(first_input_kernel, slots, last),
        "first_input",
        [piece, all_u_shape, shape(slots * ADAPTER_RANK, out_width)],
        (meta, *hbm_operands),
        [SMEM] + [ANY] * len(hbm_operands),
        [VMEM, ANY, VMEM],
        scratch_shapes=[
            pltpu.VMEM((2 * block, out_width), bf16),
            pltpu.VMEM(weight.shape, bf16),
            pltpu.VMEM(down_cols.shape, bf16),
            pltpu.VMEM((2, block, slots * ADAPTER_RANK), bf16),
            pltpu.SemaphoreType.DMA((slots + 5,)),
            pltpu.SemaphoreType.DMA((2,)),
        ],
    )
    below[last] = to_previous(grads, 0)
    for orders in ([last - 1], *[range(top, max(top - 3, -1), -1) for top in range(last - 2, -1, -3)]):
        row_parts = [part for order in orders for part in (same[order], other[order])]
        operands = (meta, weight, down_cols, up_rows, *row_parts, all_u)
        *grads, all_u = call(
            functools.partial(later_input_kernel, slots, orders),
            "later_input",
            [piece] * len(orders) + [all_u_shape],
            operands,
            [SMEM] + [VMEM] * (3 + len(row_parts)) + [ANY],
            [VMEM] * len(orders) + [ANY],
            aliases={len(operands) - 1: len(orders)},
            scratch_shapes=[
                pltpu.VMEM((2 * len(orders), block, slots * ADAPTER_RANK), bf16),
                pltpu.SemaphoreType.DMA((2 * len(orders),)),
            ],
        )
        for order, value in zip(orders, grads):
            below[order] = to_previous(value, 0)

    group = min(slots, 8)
    mixed, made = call(
        functools.partial(all_features_kernel, slots, group),
        "feature",
        [shape(slots, ADAPTER_RANK, local_width + 2 * block), token],
        (meta, saved_cols, down_cols, all_u),
        [SMEM] + [VMEM] * 3,
        [VMEM, VMEM],
        scratch_shapes=[pltpu.VMEM((count, ADAPTER_RANK, block), f32)],
    )
    row_window = call(
        functools.partial(window_kernel, slots, count),
        "row_window",
        shape(wide * block, out_width),
        (meta, *[in_hbm(v) for v in rows_in_order]),
        [SMEM] + [ANY] * count,
        VMEM,
        scratch_shapes=[pltpu.SemaphoreType.DMA((wide,))],
        late=(made,),
    )

    arrived, crossed = [None] * chips, [None] * chips
    for order in (0, *range(3, chips)):
        piece = below[order]
        arrived[order] = chip_partner(piece, order)
        crossed[order] = partner(arrived[order][1], 1)
    if chips > 2:
        below[2] = after(below[2], below[1])
    waiting = [(order, partner(below[swapped(order, count)][1], 1)) for order in (2, 1)]

    def assemble(orders, passed=None):
        operands = [meta, *[arrived[order] for order in orders], *[crossed[order] for order in orders]]
        fresh = passed is None
        return call(
            functools.partial(assemble_kernel, slots, orders),
            "assemble",
            [shape(block, count * local_width), token],
            operands if fresh else operands + [passed],
            [SMEM] + [VMEM] * (2 * len(orders)) + ([] if fresh else [HBM]),
            [HBM, VMEM],
            scratch_shapes=[pltpu.SemaphoreType.DMA((2 * len(orders),))],
            aliases={} if fresh else {len(operands): 0},
        )

    passed, _ = assemble([0, *range(3, chips)])
    mixed = lax.all_to_all(mixed, "dp", split_axis=0, concat_axis=0, tiled=True)
    down_gradient, v_block = call(
        merge_kernel,
        "merge",
        [shape(ADAPTER_RANK, count * local_width), shape(count, ADAPTER_RANK, block)],
        (mixed,),
        [VMEM],
        [VMEM, VMEM],
        late=(crossed[last], row_window),
    )
    v_all = lax.all_to_all(v_block, "dp", split_axis=0, concat_axis=0, tiled=True)
    for order, across in waiting:
        both = call(
            join_kernel,
            "join",
            shape(2, block, local_width),
            (below[order], across),
            [VMEM, VMEM],
            VMEM,
            late=(v_block,) if order == 1 else (),
        )
        both = chip_partner(both, order)
        arrived[order], crossed[order] = both, both
    passed, _ = assemble([2, 1], passed)
    up_gradient = call(
        functools.partial(up_kernel, slots),
        "up_grad",
        shape(ADAPTER_RANK, out_width),
        (meta, v_all, row_window),
        [SMEM] + [VMEM] * 2,
        VMEM,
    )
    return (passed[None], down_gradient.T[None], up_gradient.T[None])


def solution(mesh):
    return jax.shard_map(
        local,
        mesh=mesh,
        in_specs=(
            P("section", "dp", None),
            P("section", "dp", None),
            P("section", "dp", None),
            P("section", None, "dp"),
            P("section", None, "dp"),
            P("section", None),
            P("section", None),
        ),
        out_specs=(P("section", "dp", None), P("section", None, "dp"), P("section", None, "dp")),
        check_vma=False,
    )
```

```python
import functools
import math

import jax
import jax.numpy as jnp
from jax import lax
from jax.experimental import pallas as pl
from jax.experimental.pallas import tpu as pltpu
from jax.sharding import PartitionSpec as P

ADAPTER_RANK = 64
MOST = 256
MIB = 1024 * 1024

adapter_scale = 2.0

NT = (((1,), (1,)), ((), ()))
TN = (((0,), (0,)), ((), ()))
NN = (((1,), (0,)), ((), ()))

ANY = pl.BlockSpec(memory_space=pl.ANY)
HBM = pl.BlockSpec(memory_space=pltpu.MemorySpace.HBM)
SMEM = pl.BlockSpec(memory_space=pltpu.SMEM)
VMEM = pl.BlockSpec(memory_space=pltpu.VMEM)


def partner(value, distance):
    count = lax.axis_size("dp")
    return lax.ppermute(value, "dp", [(i, i ^ distance) for i in range(count)])


def chip_partner(value, order):
    count = lax.axis_size("dp")
    if count == 8 and order in (1, 2):
        pairs = [(i, i ^ (2 if (i + order) % 2 else 4)) for i in range(count)]
        return lax.ppermute(value, "dp", pairs)
    return partner(value, 2 * order) if order else value


def swapped(order, count):
    return 3 - order if count == 8 and order in (1, 2) else order


def devices_in_order(me, count):
    out = []
    for order in range(count // 2):
        distance = jnp.int32(2 * order)
        if count == 8 and order in (1, 2):
            distance = jnp.where((me + order) % 2 == 1, 2, 4)
        out += [me ^ distance, me ^ distance ^ 1]
    return jnp.stack(out).astype(jnp.int32)


def corner(value):
    if value.size <= 1 << 17:
        return value
    rows = min(16, value.shape[-2])
    tile = value[(0,) * (value.ndim - 2)][:rows, :128] if value.ndim > 2 else value[:rows, :128]
    return tile


def in_place_kernel(*refs):
    pass


def after(value, *others):
    operands = [value, *map(corner, others)]
    return pl.pallas_call(
        in_place_kernel,
        out_shape=jax.ShapeDtypeStruct(value.shape, value.dtype),
        in_specs=[ANY] * len(operands),
        out_specs=ANY,
        input_output_aliases={0: 0},
        name="in_order",
    )(*operands)


def in_hbm(value):
    return pltpu.with_memory_space_constraint(value, pltpu.MemorySpace.HBM)


def to_previous(value, distance):
    sections, count = lax.axis_size("section"), lax.axis_size("dp")
    pairs = [
        (s * count + i, (s - 1) * count + (i ^ distance))
        for s in range(1, sections)
        for i in range(count)
    ]
    return lax.ppermute(value, ("section", "dp"), pairs)


def slot_ranges(tenant_row, slot_table):
    tenants = slot_table.shape[0]
    ids = jnp.arange(tenants, dtype=jnp.int32)
    counts = jnp.sum((tenant_row[None, :] == ids[:, None]).astype(jnp.int32), axis=1)
    starts = jnp.sum((tenant_row[None, :] < ids[:, None]).astype(jnp.int32), axis=1)
    owner = slot_table[None, :] == ids[:, None]
    slot_start = jnp.sum(jnp.where(owner, starts[None, :], 0), axis=1)
    slot_count = jnp.sum(jnp.where(owner, counts[None, :], 0), axis=1)
    return slot_start, slot_count


def pick(index, refs, act):
    for k, ref in enumerate(refs):

        @pl.when(index == k)
        def _():
            act(ref)


def device_at(meta_ref, slots, place):
    return meta_ref[3 * slots + 1 + place]


def place_of(meta_ref, slots, device):
    return meta_ref[4 * slots + 1 + device]


def owned(meta_ref, slots, first_token, width):
    me = meta_ref[3 * slots]
    start, count = meta_ref[me], meta_ref[slots + me]
    token = first_token + lax.broadcasted_iota(jnp.int32, (1, width), 1)
    return (token >= start) & (token < start + count)


def slot_lanes(meta_ref, slots, rank):
    lane = lax.broadcasted_iota(jnp.int32, (1, slots * rank), 1)
    start = jnp.zeros_like(lane)
    stop = jnp.zeros_like(lane)
    for slot in range(slots):
        first = meta_ref[slot]
        inside = lane >= slot * rank
        start = jnp.where(inside, first, start)
        stop = jnp.where(inside, first + meta_ref[slots + slot], stop)
    return start, stop


class Loads:
    def __init__(self, sem):
        self.sem, self.copies = sem, {}

    def start(self, name, source, target):
        copy = pltpu.make_async_copy(source, target, self.sem.at[len(self.copies)])
        copy.start()
        self.copies[name] = copy

    def wait(self, *names):
        for name in names:
            self.copies[name].wait()


def load_input(loads, weight_ref, down_ref, weight, down):
    half = weight_ref.shape[0] // 2
    loads.start("down", down_ref, down)
    for i in range(2):
        span = pl.ds(i * half, half)
        loads.start(("weight", i), weight_ref.at[span], weight.at[span])


def write_input(loads, arriving, rows, ranks, weight, down, out_ref):
    block = out_ref.shape[1]
    half = weight.shape[0] // 2
    if arriving:
        loads.wait("down")
    for i in range(2):
        span = pl.ds(i * half, half)
        term = lax.dot_general(ranks, down[:, span], NN, preferred_element_type=jnp.float32)
        if arriving:
            loads.wait(("weight", i))
        total = lax.dot_general(rows, weight[span, :], NT, preferred_element_type=jnp.float32)
        total = (total + adapter_scale * term).astype(out_ref.dtype)
        out_ref[0, :, span], out_ref[1, :, span] = total[:block], total[block:]


def write_ranks(meta_ref, slots, order, u, lanes, held, all_u_ref, stores):
    block = held.shape[1]
    start, stop = lanes
    token = lax.broadcasted_iota(jnp.int32, (block, 1), 0)
    parts = []
    for core in range(2):
        row = pl.multiple_of(device_at(meta_ref, slots, 2 * order + core) * block, block)
        inside = (token + row >= start) & (token + row < stop)
        part = jnp.where(inside, u[core * block : (core + 1) * block], 0.0).astype(held.dtype)
        held[core] = part
        stores.start((order, core), held.at[core], all_u_ref.at[pl.ds(row, block)])
        parts.append(part)
    return jnp.concatenate(parts, axis=0)


def first_input_kernel(slots, order, meta_ref, *refs):
    row_refs, (weight_ref, down_ref, out_ref, all_u_ref, up), refs = (
        refs[:slots],
        refs[slots : slots + 5],
        refs[slots + 5 :],
    )
    rows, weight, down, held, sem, u_sem = refs
    block = out_ref.shape[1]
    rank = up.shape[0] // slots
    loads, stores = Loads(sem), Loads(u_sem)
    for k, ref in enumerate(row_refs):
        row = pl.multiple_of(device_at(meta_ref, slots, k) * rank, rank)
        loads.start(("up", k), ref.at[pl.ds(block, rank)], up.at[pl.ds(row, rank)])
    for core in range(2):
        source = row_refs[2 * order + core].at[pl.ds(0, block)]
        loads.start(("rows", core), source, rows.at[pl.ds(core * block, block)])
    load_input(loads, weight_ref, down_ref, weight, down)
    lanes = slot_lanes(meta_ref, slots, rank)
    loads.wait(*[("up", k) for k in range(slots)], ("rows", 0), ("rows", 1))
    u = lax.dot_general(rows[...], up[...], NT, preferred_element_type=jnp.float32)
    ranks = write_ranks(meta_ref, slots, order, u, lanes, held, all_u_ref, stores)
    write_input(loads, True, rows[...], ranks, weight, down, out_ref)
    stores.wait((order, 0), (order, 1))


def later_input_kernel(slots, orders, meta_ref, weight_ref, down_ref, up_ref, *refs):
    number = len(orders)
    row_refs, out_refs = refs[: 2 * number], refs[2 * number + 1 : 3 * number + 1]
    all_u_ref, held, u_sem = refs[3 * number + 1 :]
    block = out_refs[0].shape[1]
    stores = Loads(u_sem)
    lanes = slot_lanes(meta_ref, slots, up_ref.shape[0] // slots)
    for i, order in enumerate(orders):
        rows = [ref[pl.ds(0, block)] for ref in row_refs[2 * i : 2 * i + 2]]
        rows = jnp.concatenate(rows, axis=0)
        u = lax.dot_general(rows, up_ref[...], NT, preferred_element_type=jnp.float32)
        span = pl.ds(2 * i, 2)
        ranks = write_ranks(meta_ref, slots, order, u, lanes, held.at[span], all_u_ref, stores)
        write_input(None, False, rows, ranks, weight_ref, down_ref, out_refs[i])
    stores.wait(*stores.copies)


def feature_kernel(slots, rows, meta_ref, saved_ref, down_ref, u_ref, out_ref, v_ref):
    rank, block = v_ref.shape[1:]
    width = saved_ref.shape[1]
    blocks = v_ref.shape[0]
    down = down_ref[pl.ds(rows[0] * rank, len(rows) * rank), :]
    part = lax.dot_general(down, saved_ref[...], NT, preferred_element_type=jnp.float32)
    ranges = []
    for slot in rows:
        ranges.append((meta_ref[slot], meta_ref[slot] + meta_ref[slots + slot]))
    for token_block in range(blocks):
        lane = slice(token_block * block, (token_block + 1) * block)
        token = token_block * block + lax.broadcasted_iota(jnp.int32, (1, block), 1)
        value = jnp.zeros((rank, block), jnp.float32) if rows[0] == 0 else v_ref[token_block]
        for row, (start, stop) in enumerate(ranges):
            inside = (token >= start) & (token < stop)
            value = jnp.where(inside, part[row * rank : (row + 1) * rank, lane], value)
        v_ref[token_block] = value
    u = u_ref[:, pl.ds(rows[0] * rank, len(rows) * rank)]
    grad = lax.dot_general(u, saved_ref[...], TN, preferred_element_type=jnp.float32)
    grad = (adapter_scale * grad).astype(out_ref.dtype)
    for row, slot in enumerate(rows):
        out_ref[slot, :, pl.ds(0, width)] = grad[row * rank : (row + 1) * rank]


def all_features_kernel(slots, group, *refs):
    refs, token_ref = refs[:-2] + refs[-1:], refs[-2]
    token_ref[...] = jnp.zeros_like(token_ref)
    for start in range(0, slots, group):
        feature_kernel(slots, range(start, min(start + group, slots)), *refs)
    saved_ref, (out_ref, v_ref) = refs[1], refs[-2:]
    width, block = saved_ref.shape[1], v_ref.shape[2]
    value = v_ref[...]
    near = value.astype(out_ref.dtype)
    out_ref[:, :, pl.ds(width, block)] = near
    rest = value - near.astype(jnp.float32)
    out_ref[:, :, pl.ds(width + block, block)] = rest.astype(out_ref.dtype)


def join_kernel(own_ref, across_ref, out_ref):
    out_ref[0], out_ref[1] = own_ref[0], across_ref[...]


def merge_kernel(mixed_ref, down_ref, v_ref):
    count = mixed_ref.shape[0]
    block = v_ref.shape[2]
    width = mixed_ref.shape[2] - 2 * block
    total = jnp.zeros(v_ref.shape[1:], jnp.float32)
    for source in range(count):
        down_ref[:, source * width : (source + 1) * width] = mixed_ref[source, :, pl.ds(0, width)]
        for part in range(2):
            value = mixed_ref[source, :, pl.ds(width + part * block, block)]
            total = total + value.astype(jnp.float32)
    total = total.astype(v_ref.dtype)
    for target in range(count):
        v_ref[target] = total


def window_kernel(slots, count, meta_ref, *refs):
    row_refs, (out_ref, sem) = refs[:count], refs[count:]
    block = row_refs[0].shape[0] - ADAPTER_RANK
    wide = out_ref.shape[0] // block
    first = meta_ref[2 * slots + meta_ref[3 * slots]]
    for i in range(wide):
        target = out_ref.at[pl.ds(i * block, block)]
        pick(
            place_of(meta_ref, slots, first + i),
            row_refs,
            lambda ref: pltpu.make_async_copy(ref.at[pl.ds(0, block)], target, sem.at[i]).start(),
        )
    for i in range(wide):
        target = out_ref.at[pl.ds(i * block, block)]
        pltpu.make_async_copy(row_refs[0].at[pl.ds(0, block)], target, sem.at[i]).wait()


def up_kernel(slots, meta_ref, v_ref, window_ref, out_ref):
    block = v_ref.shape[2]
    span = window_ref.shape[0]
    me = meta_ref[3 * slots]
    first = meta_ref[2 * slots + me]
    values = [v_ref[first + i] for i in range(span // block)]
    values = jnp.concatenate(values, axis=1)
    values = jnp.where(owned(meta_ref, slots, first * block, span), values, jnp.zeros_like(values))
    product = lax.dot_general(values, window_ref[...], NN, preferred_element_type=jnp.float32)
    out_ref[...] = (adapter_scale * product).astype(out_ref.dtype)


def regroup_kernel(in_ref, out_ref):
    width = out_ref.shape[2]
    for k in range(out_ref.shape[0]):
        out_ref[k] = in_ref[:, k * width : (k + 1) * width]


def assemble_kernel(slots, orders, meta_ref, *refs):
    own_refs, other_refs = refs[: len(orders)], refs[len(orders) : 2 * len(orders)]
    out_ref, token_ref, sem = refs[-3:]
    token_ref[...] = jnp.zeros_like(token_ref)
    width = own_refs[0].shape[-1]
    copies = []
    for order, own_ref, other_ref in zip(orders, own_refs, other_refs):
        own_ref = own_ref.at[0]
        other = 2 * swapped(order, slots) + 1
        if len(other_ref.shape) == 3:
            other, other_ref = 2 * order + 1, other_ref.at[1]
        for source, ref in ((2 * order, own_ref), (other, other_ref)):
            column = pl.multiple_of(device_at(meta_ref, slots, source) * width, width)
            target = out_ref.at[:, pl.ds(column, width)]
            copies.append(pltpu.make_async_copy(ref, target, sem.at[len(copies)]))
    for copy in copies:
        copy.start()
    for copy in copies:
        copy.wait()


def local(
    output_gradient,
    saved_input,
    frozen_matrix,
    adapter_down_maps,
    adapter_up_maps,
    token_tenants,
    tenant_slot_lookup,
):
    grad_rows = output_gradient[0]
    saved_rows = saved_input[0]
    weight = frozen_matrix[0]
    down_local = adapter_down_maps[0].T
    up_local = adapter_up_maps[0].T
    slots = tenant_slot_lookup.shape[1]
    block, out_width = grad_rows.shape
    local_width = weight.shape[0]
    count = lax.axis_size("dp")
    chips = count // 2
    wide = -(-MOST // block) + 1
    me = lax.axis_index("dp").astype(jnp.int32)
    bf16, f32 = jnp.bfloat16, jnp.float32

    slot_start, slot_count = slot_ranges(token_tenants[0], tenant_slot_lookup[0])
    first = jnp.minimum(slot_start // block, count - wide)
    devices = devices_in_order(me, count)
    ids = jnp.arange(count, dtype=jnp.int32)
    places = jnp.sum(jnp.where(devices[None, :] == ids[:, None], ids[None, :], 0), axis=1)
    meta = [slot_start, slot_count, first, me[None], devices, places]
    meta = jnp.concatenate(meta).astype(jnp.int32)

    def call(kernel, name, out, operands, in_specs, out_specs, scratch_shapes=(), aliases=None, late=()):
        arrays = list(operands) + (out if isinstance(out, list) else [out])
        held = sum(v.size * v.dtype.itemsize for v in arrays)
        held += sum(
            math.prod(v.shape) * jnp.dtype(v.dtype).itemsize
            for v in scratch_shapes
            if v.memory_space == pltpu.VMEM
        )
        number = len(operands)

        def body(*refs):
            kernel(*refs[:number], *refs[number + len(late) :])

        return pl.pallas_call(
            body,
            out_shape=out,
            in_specs=list(in_specs) + [ANY] * len(late),
            out_specs=out_specs,
            scratch_shapes=scratch_shapes,
            input_output_aliases=aliases or {},
            compiler_params=pltpu.CompilerParams(vmem_limit_bytes=min(60 * MIB, 2 * held + 4 * MIB)),
            name=name,
            cost_estimate=pl.CostEstimate(flops=0, bytes_accessed=0, transcendentals=0),
        )(*operands, *map(corner, late))

    def shape(*dims, dtype=bf16):
        return jax.ShapeDtypeStruct(dims, dtype)

    token = shape(8, 128, dtype=f32)

    last = chips - 1
    rows = jnp.concatenate([grad_rows, up_local], axis=0)
    if chips == 4:
        same = [chip_partner(rows, order) for order in range(3)]
        same.append(chip_partner(same[1], 2))
    else:
        same = [chip_partner(rows, order) for order in range(chips)]
    other = [partner(same[swapped(order, count)], 1) for order in range(chips)]
    rows_in_order = [part for pair in zip(same, other) for part in pair]

    def regroup(name, value):
        pieces = shape(count, value.shape[0], local_width)
        return call(regroup_kernel, name, pieces, (value,), [VMEM], VMEM)

    down_pieces = regroup("regroup_down", down_local)
    saved_pieces = regroup("regroup_saved", saved_rows)
    down_cols = lax.all_to_all(down_pieces, "dp", split_axis=0, concat_axis=0, tiled=True)
    down_cols = down_cols.reshape(slots * ADAPTER_RANK, local_width)
    saved_cols = lax.all_to_all(
        after(saved_pieces, down_cols, same[last]), "dp", split_axis=0, concat_axis=0, tiled=True
    ).reshape(count * block, local_width)

    below = [None] * chips
    hbm_operands = [in_hbm(v) for v in (*rows_in_order, weight, down_cols)]
    all_u_shape = shape(count * block, slots * ADAPTER_RANK)
    piece = shape(2, block, local_width)
    grads, all_u, up_rows = call(
        functools.partial(first_input_kernel, slots, last),
        "first_input",
        [piece, all_u_shape, shape(slots * ADAPTER_RANK, out_width)],
        (meta, *hbm_operands),
        [SMEM] + [ANY] * len(hbm_operands),
        [VMEM, ANY, VMEM],
        scratch_shapes=[
            pltpu.VMEM((2 * block, out_width), bf16),
            pltpu.VMEM(weight.shape, bf16),
            pltpu.VMEM(down_cols.shape, bf16),
            pltpu.VMEM((2, block, slots * ADAPTER_RANK), bf16),
            pltpu.SemaphoreType.DMA((slots + 5,)),
            pltpu.SemaphoreType.DMA((2,)),
        ],
    )
    below[last] = to_previous(grads, 0)
    for orders in ([last - 1], *[range(top, max(top - 3, -1), -1) for top in range(last - 2, -1, -3)]):
        row_parts = [part for order in orders for part in (same[order], other[order])]
        operands = (meta, weight, down_cols, up_rows, *row_parts, all_u)
        *grads, all_u = call(
            functools.partial(later_input_kernel, slots, orders),
            "later_input",
            [piece] * len(orders) + [all_u_shape],
            operands,
            [SMEM] + [VMEM] * (3 + len(row_parts)) + [ANY],
            [VMEM] * len(orders) + [ANY],
            aliases={len(operands) - 1: len(orders)},
            scratch_shapes=[
                pltpu.VMEM((2 * len(orders), block, slots * ADAPTER_RANK), bf16),
                pltpu.SemaphoreType.DMA((2 * len(orders),)),
            ],
        )
        for order, value in zip(orders, grads):
            below[order] = to_previous(value, 0)

    group = min(slots, 8)
    mixed, made = call(
        functools.partial(all_features_kernel, slots, group),
        "feature",
        [shape(slots, ADAPTER_RANK, local_width + 2 * block), token],
        (meta, saved_cols, down_cols, all_u),
        [SMEM] + [VMEM] * 3,
        [VMEM, VMEM],
        scratch_shapes=[pltpu.VMEM((count, ADAPTER_RANK, block), f32)],
    )
    row_window = call(
        functools.partial(window_kernel, slots, count),
        "row_window",
        shape(wide * block, out_width),
        (meta, *[in_hbm(v) for v in rows_in_order]),
        [SMEM] + [ANY] * count,
        VMEM,
        scratch_shapes=[pltpu.SemaphoreType.DMA((wide,))],
        late=(made,),
    )

    arrived, crossed = [None] * chips, [None] * chips
    for order in (0, *range(3, chips)):
        piece = below[order]
        arrived[order] = chip_partner(piece, order)
        crossed[order] = partner(arrived[order][1], 1)
    if chips > 2:
        below[2] = after(below[2], below[1])
    waiting = [(order, partner(below[swapped(order, count)][1], 1)) for order in (2, 1)]

    def assemble(orders, passed=None):
        operands = [meta, *[arrived[order] for order in orders], *[crossed[order] for order in orders]]
        fresh = passed is None
        return call(
            functools.partial(assemble_kernel, slots, orders),
            "assemble",
            [shape(block, count * local_width), token],
            operands if fresh else operands + [passed],
            [SMEM] + [VMEM] * (2 * len(orders)) + ([] if fresh else [HBM]),
            [HBM, VMEM],
            scratch_shapes=[pltpu.SemaphoreType.DMA((2 * len(orders),))],
            aliases={} if fresh else {len(operands): 0},
        )

    mixed = lax.all_to_all(mixed, "dp", split_axis=0, concat_axis=0, tiled=True)
    down_gradient, v_block = call(
        merge_kernel,
        "merge",
        [shape(ADAPTER_RANK, count * local_width), shape(count, ADAPTER_RANK, block)],
        (mixed,),
        [VMEM],
        [VMEM, VMEM],
        late=(crossed[last], row_window),
    )
    v_all = lax.all_to_all(v_block, "dp", split_axis=0, concat_axis=0, tiled=True)
    for order, across in waiting:
        both = call(
            join_kernel,
            "join",
            shape(2, block, local_width),
            (below[order], across),
            [VMEM, VMEM],
            VMEM,
            late=(v_block,) if order == 1 else (),
        )
        both = chip_partner(both, order)
        arrived[order], crossed[order] = both, both
    passed, _ = assemble([*range(chips)])
    up_gradient = call(
        functools.partial(up_kernel, slots),
        "up_grad",
        shape(ADAPTER_RANK, out_width),
        (meta, v_all, row_window),
        [SMEM] + [VMEM] * 2,
        VMEM,
    )
    return (passed[None], down_gradient.T[None], up_gradient.T[None])


def solution(mesh):
    return jax.shard_map(
        local,
        mesh=mesh,
        in_specs=(
            P("section", "dp", None),
            P("section", "dp", None),
            P("section", "dp", None),
            P("section", None, "dp"),
            P("section", None, "dp"),
            P("section", None),
            P("section", None),
        ),
        out_specs=(P("section", "dp", None), P("section", None, "dp"), P("section", None, "dp")),
        check_vma=False,
    )
```
